32 devices in a mesh: energy: 8 (over z, x), space: 4 (over y, core).
Axes of the slice: x: 2, y: 2, z: 4, core: 2. Of those that a mesh axis runs over, the one named last changes fastest.
Arguments:
- lesser_prev: float32 [2, 8, 4, 128, 128], P(None, 'energy', 'space'), may hold values from -6 to 6
- retarded: float32 [2, 8, 4, 128, 128], P(None, 'energy', 'space'), may hold values from -1.5 to 1.5, as said below
- coupling: float32 [2, 4, 128, 128], P(None, 'space'), may hold values from -1.5 to 1.5, as said below
- gradient_table: float32 [4, 2, 128, 128], replicated, may hold values from -0.5 to 0.5
- material: int32 [4], replicated, may hold values from 0 to 3
- offsets: int32 [8], replicated, may hold values from -2 to 2
- weights: float32 [8], replicated, may hold values from 0.05 to 0.3
Outputs:
- lesser_left: float32 [2, 8, 4, 128, 128], P(None, 'energy', 'space')
The draws below stay inside these ranges and needn't reach their ends.
Inputs may be any that keep to these rules, and one draw needn't show every extreme that they name: `retarded`: each block is a complex diagonal of modulus below one plus small full-rank noise. `coupling`: each block is the identity plus small full-rank complex noise.
All inputs are finite; a program needn't handle non-finite values.
Results may differ from the reference program's by a relative error of at most 0.0001.
Values sent between devices are 32-bit elements; how exact they have to be, the bound alone decides.
No kernel may reach another device: no remote copies, remote signals or barrier semaphores. Data moves between devices by JAX's collectives and lax.ppermute only.
A program may use at most 64 MiB of HBM per device.

```python
import math
import jax
import jax.numpy as jnp
from jax import lax

BLOCK = 128
MODES = 8
KINDS = 4
NE = 8
NSLAB = 4


def roughness(key, shape):
    return jnp.clip(jax.random.normal(key, shape, jnp.float32), -4.0, 4.0)


def draw_retarded(key, part):
    rate_key, phase_key, noise_key = jax.random.split(jax.random.fold_in(key, 11), 3)
    log_loss = jax.random.uniform(rate_key, (NE, 1, BLOCK), jnp.float32, math.log(0.03), math.log(0.5))
    modulus = 1.0 - jnp.exp(log_loss)
    phase = jax.random.uniform(phase_key, (NE, 1, BLOCK), jnp.float32, -math.pi, math.pi)
    identity = jnp.eye(BLOCK, dtype=jnp.float32)
    real_diag = (modulus * jnp.cos(phase))[..., None] * identity
    imag_diag = (modulus * jnp.sin(phase))[..., None] * identity
    diagonal = jnp.stack([real_diag, imag_diag])
    noise = roughness(noise_key, (2, NE, NSLAB, BLOCK, BLOCK)) * (0.1 / math.sqrt(BLOCK))
    return diagonal + noise


def draw_coupling(key, part):
    noise_key = jax.random.fold_in(key, 23)
    identity = jnp.eye(BLOCK, dtype=jnp.float32)
    base = jnp.stack([identity, jnp.zeros_like(identity)])[:, None]
    noise = roughness(noise_key, (2, NSLAB, BLOCK, BLOCK)) * (0.1 / math.sqrt(BLOCK))
    return base + noise


def plant(entries, rng, smallest, high):
    index_at = [jax.random.randint(jax.random.fold_in(rng, axis), (), 0, length) for axis, length in enumerate(entries.shape)]
    main_axis = entries.shape.index(max(entries.shape))
    neighbour = index_at[:main_axis] + [(index_at[main_axis] + 1) % entries.shape[main_axis]] + index_at[main_axis + 1:]
    return entries.at[tuple(index_at)].set(smallest).at[tuple(neighbour)].set(high)


def steps_of(stream_key, extent, cuts, least, largest):
    loudness = 1.0
    for position, shards_of in cuts:
        draws = jax.random.uniform(jax.random.fold_in(jax.random.fold_in(stream_key, 6), position), (shards_of,), jnp.float32, least / len(cuts), largest / len(cuts))
        loudness = loudness * jnp.repeat(jnp.exp(draws), extent[position] // shards_of).reshape((-1,) + (1,) * (len(extent) - 1 - position))
    return loudness


def bell_draw(key, dims, spread, limit, cuts=(), kind=jnp.bfloat16):
    factor_of = steps_of(key, dims, cuts, -0.22, 0.18) if cuts else 1.0
    values = jax.random.normal(key, dims, jnp.float32) * spread * factor_of
    return jnp.minimum(jnp.maximum(values, -limit), limit).astype(kind)


def setup_inputs(seed: int = 0) -> dict:
    streams_of = jax.random.split(jax.random.key(seed), 8)
    lesser_prev = bell_draw(streams_of[0], (2, NE, NSLAB, BLOCK, BLOCK), 1.0, 6.0, ((1, 8), (2, 4)), jnp.float32)
    retarded = draw_retarded(jax.random.fold_in(streams_of[7], 71), 0)
    coupling = draw_coupling(jax.random.fold_in(streams_of[7], 71), 0)
    gradient_table = bell_draw(streams_of[3], (KINDS, 2, BLOCK, BLOCK), BLOCK ** -0.5, 0.5, (), jnp.float32)
    material = plant(jax.random.randint(streams_of[4], (NSLAB,), 0, KINDS), jax.random.fold_in(streams_of[4], 1), 0, KINDS - 1).astype(jnp.int32)
    offsets = plant(jax.random.randint(streams_of[5], (MODES,), 0 - NE // 4, NE // 4 + 1), jax.random.fold_in(streams_of[5], 1), 0 - NE // 4, (NE // 4 + 1) - 1).astype(jnp.int32)
    weights = jnp.clip(jnp.exp(jax.random.uniform(streams_of[6], (MODES,), jnp.float32, math.log(0.05), math.log(0.3))), 0.05, 0.3)
    return dict(lesser_prev=lesser_prev, retarded=retarded, coupling=coupling, gradient_table=gradient_table, material=material, offsets=offsets, weights=weights)


HIGHEST_PRECISION = lax.Precision.HIGHEST


def real_product(left, right):
    return jnp.matmul(left, right, precision=HIGHEST_PRECISION)


def complex_product(left, right):
    real_part = real_product(left[0], right[0]) - real_product(left[1], right[1])
    imag_part = real_product(left[0], right[1]) + real_product(left[1], right[0])
    return jnp.stack([real_part, imag_part])


def dagger(matrix):
    return jnp.stack([jnp.swapaxes(matrix[0], -1, -2), -jnp.swapaxes(matrix[1], -1, -2)])


def phonon_matrix(offsets, weights, count):
    grid = jnp.arange(count, dtype=jnp.int32)
    hits = (grid[None, None, :] == grid[None, :, None] + offsets[:, None, None]).astype(jnp.float32)
    return jnp.einsum("k,kef->ef", weights, hits, precision=HIGHEST_PRECISION)


def reference(lesser_prev, retarded, coupling, gradient_table, material, offsets, weights):
    picks = (material[:, None] == jnp.arange(KINDS, dtype=jnp.int32)[None, :]).astype(jnp.float32)
    links = jnp.einsum("sk,kcab->csab", picks, gradient_table, precision=HIGHEST_PRECISION)
    links_before = jnp.concatenate([links[:, :1], links[:, :-1]], axis=1)

    def neighbour_terms(slab_field):
        zero_slab = jnp.zeros_like(slab_field[:, :1])
        after_field = jnp.concatenate([slab_field[:, 1:], zero_slab], axis=1)
        before_field = jnp.concatenate([zero_slab, slab_field[:, :-1]], axis=1)
        right_term = complex_product(complex_product(links, after_field), dagger(links))
        left_term = complex_product(complex_product(dagger(links_before), before_field), links_before)
        return slab_field + right_term + left_term

    mixed = lax.map(neighbour_terms, jnp.moveaxis(lesser_prev, 1, 0))
    kernel = phonon_matrix(offsets, weights, NE)
    sigma = jnp.einsum("ef,fcsab->ecsab", kernel, mixed, precision=HIGHEST_PRECISION)

    def sweep(package):
        sigma_energy, retarded_energy = package
        gain = complex_product(retarded_energy, coupling)
        source = complex_product(complex_product(retarded_energy, sigma_energy), dagger(retarded_energy))

        def advance(state, item):
            slab_gain, slab_source = item
            state = complex_product(complex_product(slab_gain, state), dagger(slab_gain)) + slab_source
            return state, state

        initial = jnp.zeros((2, BLOCK, BLOCK), jnp.float32)
        _, states = lax.scan(advance, initial, (jnp.moveaxis(gain, 1, 0), jnp.moveaxis(source, 1, 0)))
        return jnp.moveaxis(states, 0, 1)

    result = lax.map(sweep, (sigma, jnp.moveaxis(retarded, 1, 0)))
    return jnp.moveaxis(result, 0, 1)
```

```python
import functools

import jax
import jax.numpy as jnp
from jax import lax
from jax.experimental import pallas as pl
from jax.experimental.pallas import tpu as pltpu
from jax.sharding import PartitionSpec as P

F32 = jnp.float32
BF16 = jnp.bfloat16
VMEM = pl.BlockSpec(memory_space=pltpu.VMEM)
SMEM = pl.BlockSpec(memory_space=pltpu.SMEM)
NN = (((1,), (0,)), ((), ()))
NT = (((1,), (1,)), ((), ()))


def split(value):
    high = value.astype(BF16)
    return high, (value - high.astype(F32)).astype(BF16)


def rows(block):
    return jnp.concatenate([block[0], block[1]], axis=1)


def full(row):
    half = row.shape[1] // 2
    turned = jnp.concatenate([-row[:, half:], row[:, :half]], axis=1)
    return jnp.concatenate([row, turned], axis=0)


def product(left, right, dims):
    def dot(a, b):
        return lax.dot_general(a, b, dims, preferred_element_type=F32)

    return dot(left[0], right[0]) + (dot(left[0], right[1]) + dot(left[1], right[0]))


def times(left, right_block):
    return product(left, [full(part) for part in split(rows(right_block))], NN)


def times_dagger(left, right_block):
    return product(left, [full(part) for part in split(rows(right_block))], NT)


def smear_kernel(group, offsets, weights, own, other_a, other_b, *outs):
    count = lax.axis_size("energy")
    mine = lax.axis_index("energy")
    place, rank = mine // group, mine % group
    source_a, source_b, has_a, has_b = partners(place, count // group, mine, group)

    def coefficient(target, source, valid):
        total = jnp.float32(0)
        for mode in range(offsets.shape[0]):
            total += jnp.where(target + offsets[mode] == source, weights[mode], jnp.float32(0))
        return jnp.where(valid, total, jnp.float32(0))

    for step in range(group):
        target = place * group + (rank + step) % group
        outs[step][...] = (
            coefficient(target, mine, True) * own[...]
            + coefficient(target, source_a, has_a) * other_a[...]
            + coefficient(target, source_b, has_b) * other_b[...]
        )


def partners(place, places, mine, group):
    even = place % 2 == 0
    side_a = jnp.where(even, 1, -1)
    has_a = (place + side_a < places) & (place + side_a >= 0)
    has_b = (place - side_a < places) & (place - side_a >= 0)
    return mine + side_a * group, mine - side_a * group, has_a, has_b


def matchings(places, group):
    result = []
    for first in (0, 1):
        pairs = []
        for place in range(places):
            other = place + 1 if place % 2 == first else place - 1
            for rank in range(group):
                mine = place * group + rank
                if 0 <= other < places:
                    pairs.append((mine, other * group + rank))
                elif group % 2 == 0:
                    pairs.append((mine, mine ^ 1))
        result.append(pairs)
    return result


def factor_kernel(count, material, table, *refs):
    retarded, coupling, outs = refs[:count], refs[count : 2 * count], refs[2 * count : 2 * count + 2]
    held_r, held_c = refs[2 * count + 2 :]
    mine = lax.axis_index("space")
    size = table.shape[-1]
    for slot in range(count):
        held_r[slot] = retarded[slot][...]
        held_c[slot] = coupling[slot][...]

    def store(slab, which, value, valid):
        slot = jnp.bitwise_xor(mine, lax.rem(slab + count, count))
        value = jnp.where(valid, value, jnp.float32(0))
        for out, part in zip(outs, split(value)):
            out[slot, which * size : (which + 1) * size] = part

    def step(index, state):
        slab = mine - index
        here = jnp.maximum(slab, 0)
        before = jnp.maximum(slab - 1, 0)
        parts = split(state)
        store(slab, 0, state, slab >= 0)
        store(slab + 1, 1, times(parts, table[material[here]]), (slab >= 0) & (slab + 1 < count))
        store(slab - 1, 2, times_dagger(parts, table[material[before]]), slab >= 1)
        carried = times(parts, held_c[jnp.bitwise_xor(mine, here)])
        return times(split(carried), held_r[jnp.bitwise_xor(mine, before)])

    state = rows(held_r[0])
    if count <= 4:
        for index in range(count):
            state = step(index, state)
    else:
        lax.fori_loop(0, count, step, state)


def field_kernel(slots, has_start, *refs):
    fields, (high, low), rest = refs[: len(slots)], refs[len(slots) : len(slots) + 2], refs[len(slots) + 2 :]
    out = rest[-1]
    size = out.shape[-1]
    total = rows(rest[0]) if has_start else None
    for field, slot in zip(fields, slots):
        factors = (high[slot], low[slot])
        left = split(times(factors, field))
        for which in range(3):
            part = slice(which * size, (which + 1) * size)
            term = product([p[part] for p in left], [full(f[part]) for f in factors], NT)
            total = term if total is None else total + term
    out[0] = total[:, :size]
    out[1] = total[:, size:]


def call(kernel, shapes, specs, *args, scratch=(), flops=0):
    return pl.pallas_call(
        kernel,
        out_shape=shapes,
        in_specs=specs,
        out_specs=jax.tree.map(lambda _: VMEM, shapes),
        scratch_shapes=scratch,
        compiler_params=pltpu.CompilerParams(vmem_limit_bytes=32 * 2**20),
        cost_estimate=pl.CostEstimate(
            flops=flops, bytes_accessed=sum(a.size * a.dtype.itemsize for a in args), transcendentals=0
        ),
    )(*args)


def exchange(value, bit):
    count = lax.axis_size("space")
    return lax.ppermute(value, "space", [(i, i ^ bit) for i in range(count)])


def gather(slots, bits):
    for bit in bits:
        keys = list(slots)
        moved = exchange(jnp.concatenate([slots[key] for key in keys], axis=0), bit)
        parts = jnp.split(moved, len(keys), axis=0)
        slots = slots | {key ^ bit: part for key, part in zip(keys, parts)}
    return slots


def per_device(lesser_prev, retarded, coupling, gradient_table, material, offsets, weights):
    size = lesser_prev.shape[-1]
    energies, slabs = lax.axis_size("energy"), lax.axis_size("space")
    group = max(energies // 4, 1)
    block = jax.ShapeDtypeStruct((2, size, size), F32)
    own = lesser_prev.reshape(2, size, size)
    chip_bits = [1 << b for b in range(1, slabs.bit_length() - 1)]

    pairs_a, pairs_b = matchings(energies // group, group)
    other_a = lax.ppermute(own, "energy", pairs_a)
    other_b = lax.ppermute(own, "energy", pairs_b)
    packed = jnp.concatenate([retarded.reshape(2, size, size), coupling.reshape(2, size, size)], axis=0)
    packed = gather({0: packed}, chip_bits + [1])

    sums = call(
        functools.partial(smear_kernel, group), [block] * group, [SMEM, SMEM, VMEM, VMEM, VMEM],
        offsets, weights, own, other_a, other_b,
    )
    if group == 2 and len(chip_bits) == 1:
        bit = chip_bits[0]
        both = [
            (e * slabs + s, (e ^ 1) * slabs + (s ^ bit)) for e in range(energies) for s in range(slabs)
        ]
        far = lax.ppermute(sums[1], ("energy", "space"), both)
        near = lax.ppermute(sums[1], "energy", [(e, e ^ 1) for e in range(energies)])
        across = exchange(sums[0], bit)
        fields = {0: sums[0] + near, bit: across + far}
    else:
        field = sums[0]
        for step in range(1, group):
            pairs = [(e, e - e % group + (e + step) % group) for e in range(energies)]
            field = field + lax.ppermute(sums[step], "energy", pairs)
        fields = gather({0: field}, chip_bits)
    early = list(fields)
    fields = gather(fields, [1])
    late = [slot for slot in fields if slot not in early]

    order = range(slabs)
    factor_shape = jax.ShapeDtypeStruct((slabs, 3 * size, 2 * size), BF16)
    factors = call(
        functools.partial(factor_kernel, slabs), [factor_shape] * 2, [SMEM] + [VMEM] * (2 * slabs + 1),
        material, gradient_table, *[packed[s][:2] for s in order], *[packed[s][2:] for s in order],
        scratch=[pltpu.VMEM((slabs, 2, size, size), F32)] * 2, flops=10**9,
    )
    first = call(
        functools.partial(field_kernel, early, False), block, [VMEM] * (len(early) + 2),
        *[fields[s] for s in early], *factors, flops=10**9,
    )
    state = call(
        functools.partial(field_kernel, late, True), block, [VMEM] * (len(late) + 3),
        *[fields[s] for s in late], *factors, first, flops=10**9,
    )
    return state.reshape(lesser_prev.shape)


def solution(mesh):
    placed = (
        P(None, "energy", "space", None, None),
        P(None, "energy", "space", None, None),
        P(None, "space", None, None),
        P(),
        P(),
        P(),
        P(),
    )
    return jax.shard_map(
        per_device,
        mesh=mesh,
        in_specs=placed,
        out_specs=P(None, "energy", "space", None, None),
        check_vma=False,
    )
```

```python
import functools

import jax
import jax.numpy as jnp
from jax import lax
from jax.experimental import pallas as pl
from jax.experimental.pallas import tpu as pltpu
from jax.sharding import PartitionSpec as P

F32 = jnp.float32
BF16 = jnp.bfloat16
VMEM = pl.BlockSpec(memory_space=pltpu.VMEM)
SMEM = pl.BlockSpec(memory_space=pltpu.SMEM)
NN = (((1,), (0,)), ((), ()))
NT = (((1,), (1,)), ((), ()))


def split(value):
    high = value.astype(BF16)
    return high, (value - high.astype(F32)).astype(BF16)


def rows(block):
    return jnp.concatenate([block[0], block[1]], axis=1)


def block_of(row):
    half = row.shape[1] // 2
    return jnp.stack([row[:, :half], row[:, half:]])


def full(row):
    half = row.shape[1] // 2
    turned = jnp.concatenate([-row[:, half:], row[:, :half]], axis=1)
    return jnp.concatenate([row, turned], axis=0)


def product(left, right, dims):
    def dot(a, b):
        return lax.dot_general(a, b, dims, preferred_element_type=F32)

    return dot(left[0], right[0]) + (dot(left[0], right[1]) + dot(left[1], right[0]))


def times(left, right_block):
    return product(left, [full(part) for part in split(rows(right_block))], NN)


def times_dagger(left, right_block):
    return product(left, [full(part) for part in split(rows(right_block))], NT)


def share_kernel(group, offsets, weights, out):
    count = lax.axis_size("energy")
    mine = lax.axis_index("energy")
    place, rank = mine // group, mine % group
    source_a, source_b, has_a, has_b = partners(place, count // group, mine, group)

    def coefficient(target, source, valid):
        total = jnp.float32(0)
        for mode in range(offsets.shape[0]):
            total += jnp.where(target + offsets[mode] == source, weights[mode], jnp.float32(0))
        return jnp.where(valid, total, jnp.float32(0))

    for step in range(group):
        target = place * group + (rank + step) % group
        for index, (source, valid) in enumerate(((mine, True), (source_a, has_a), (source_b, has_b))):
            out[step, index] = jnp.full(out.shape[2:], coefficient(target, source, valid), F32)


def smear_kernel(group, shares, own, other_a, other_b, *outs):
    shape = (-1,) + shares.shape[2:]
    parts = [part[...].reshape(shape) for part in (own, other_a, other_b)]
    for step in range(group):
        total = sum(shares[step, index][None] * part for index, part in enumerate(parts))
        outs[step][...] = total.reshape(outs[step].shape)


def partners(place, places, mine, group):
    even = place % 2 == 0
    side_a = jnp.where(even, 1, -1)
    has_a = (place + side_a < places) & (place + side_a >= 0)
    has_b = (place - side_a < places) & (place - side_a >= 0)
    return mine + side_a * group, mine - side_a * group, has_a, has_b


def matchings(places, group):
    result = []
    for first in (0, 1):
        pairs = []
        for place in range(places):
            other = place + 1 if place % 2 == first else place - 1
            for rank in range(group):
                mine = place * group + rank
                if 0 <= other < places:
                    pairs.append((mine, other * group + rank))
                elif group % 2 == 0:
                    pairs.append((mine, mine ^ 1))
        result.append(pairs)
    return result


def pair_kernel(own, other, out):
    odd = lax.axis_index("space") % 2 == 1
    mine, theirs = own[...], other[...]
    first, second = jnp.where(odd, theirs, mine), jnp.where(odd, mine, theirs)
    out[0:2] = block_of(times(split(times(split(rows(second[:2])), second[2:])), first[:2]))
    out[2:4] = second[:2]
    if out.shape[0] > 4:
        out[4:6] = first[2:]


def valid_terms(slab, mine, count):
    return slab <= mine, (slab >= 1) & (slab <= mine + 1), slab < mine


def factor_kernel(count, material, table, own, other, *refs):
    pairs = refs[: count // 2]
    outs, token, held, base = refs[count // 2 : count // 2 + 2], *refs[count // 2 + 2 :]
    mine = lax.axis_index("space")
    size = table.shape[-1]
    for slot in range(1, count // 2):
        held[slot - 1] = pairs[slot][...]
    token[...] = jnp.zeros_like(token)

    def store(slab, which, parts):
        valid = valid_terms(slab, mine, count)
        position = sum((v.astype(jnp.int32) for v in valid[:which]), jnp.int32(0))

        @pl.when(valid[which] & (slab >= 0) & (slab < count))
        def _():
            for out, part in zip(outs, parts):
                out[jnp.bitwise_xor(mine, slab), pl.ds(pl.multiple_of(position * size, size), size)] = part

    def spread(slabs, maps):
        made = []
        for slab, whole in zip(slabs, maps):
            parts = split(whole)
            right = times(parts, table[material[slab]])
            left = times_dagger(parts, table[material[jnp.maximum(slab - 1, 0)]])
            made.append((parts, split(right), split(left)))
        for slab, (same, right, left) in zip(slabs, made):
            store(slab, 0, same)
            store(slab + 1, 1, right)
            store(slab - 1, 2, left)

    odd = mine % 2 == 1

    @pl.when(odd)
    def _():
        spread([mine, mine - 1], [rows(own[:2]), rows(pairs[0][:2])])

    @pl.when(jnp.logical_not(odd))
    def _():
        spread([mine], [rows(own[:2])])

    @pl.when(mine >= 2)
    def _():
        start = split(jnp.where(odd, rows(pairs[0][:2]), rows(own[:2])))
        base[...] = times(start, jnp.where(odd, other[2:], own[2:]))

    def earlier(step, _):
        pair = mine // 2 - step
        block = held.at[jnp.bitwise_xor(mine // 2, pair) - 1]
        parts = split(base[...])
        near, far = times(parts, block[2:4]), times(parts, block[0:2])
        spread([2 * pair + 1, 2 * pair], [near, far])
        if held.shape[1] > 4:
            base[...] = times(split(far), block[4:6])
        return _

    lax.fori_loop(1, mine // 2 + 1, earlier, 0)


def add_kernel(left, right, after, out):
    out[...] = left[...] + right[...]


def field_kernel(count, slot, has_state, field, high, low, *rest):
    out = rest[-1]
    size = out.shape[-1]
    mine = lax.axis_index("space")
    valid = valid_terms(jnp.bitwise_xor(mine, slot), mine, count)
    present = sum(v.astype(jnp.int32) for v in valid)

    def run(terms):
        total = rows(rest[0]) if has_state else jnp.zeros((size, 2 * size), F32)
        if terms:
            factors = [part[slot, : terms * size] for part in (high, low)]
            left = split(times(factors, field))
            for term in range(terms):
                here = slice(term * size, (term + 1) * size)
                total = total + product([p[here] for p in left], [full(f[here]) for f in factors], NT)
        out[...] = block_of(total)

    for terms in range(4):
        pl.when(present == terms)(functools.partial(run, terms))


def call(kernel, shapes, specs, *args, scratch=()):
    return pl.pallas_call(
        kernel,
        out_shape=shapes,
        in_specs=specs,
        out_specs=jax.tree.map(lambda _: VMEM, shapes),
        scratch_shapes=scratch,
        compiler_params=pltpu.CompilerParams(vmem_limit_bytes=32 * 2**20),
        cost_estimate=pl.CostEstimate(
            flops=10**9, bytes_accessed=sum(a.size * a.dtype.itemsize for a in args), transcendentals=0
        ),
    )(*args)


def exchange(value, bit):
    count = lax.axis_size("space")
    return lax.ppermute(value, "space", [(i, i ^ bit) for i in range(count)])


def gather(slots, bits):
    for bit in bits:
        slots = slots | {key ^ bit: exchange(block, bit) for key, block in slots.items()}
    return slots


def per_device(lesser_prev, retarded, coupling, gradient_table, material, offsets, weights):
    size = lesser_prev.shape[-1]
    energies, slabs = lax.axis_size("energy"), lax.axis_size("space")
    group = max(energies // 4, 1)
    block = jax.ShapeDtypeStruct((2, size, size), F32)
    own = lesser_prev.reshape(2, size, size)
    chip_bits = [1 << b for b in range(1, slabs.bit_length() - 1)]

    pairs_a, pairs_b = matchings(energies // group, group)
    other_a = lax.ppermute(own, "energy", pairs_a)
    other_b = lax.ppermute(own, "energy", pairs_b)
    packed = jnp.concatenate([retarded.reshape(2, size, size), coupling.reshape(2, size, size)], axis=0)
    packed_other = exchange(packed, 1)
    kept = 4 if slabs <= 4 else 6
    pair = call(pair_kernel, jax.ShapeDtypeStruct((kept, size, size), F32), [VMEM] * 2, packed, packed_other)
    pairs = gather({0: pair}, chip_bits)
    factor_shape = jax.ShapeDtypeStruct((slabs, 3 * size, 2 * size), BF16)
    *factors, token = call(
        functools.partial(factor_kernel, slabs), [factor_shape] * 2 + [jax.ShapeDtypeStruct((8, 128), F32)],
        [SMEM] + [VMEM] * (3 + slabs // 2),
        material, gradient_table, packed, packed_other, *[pairs[2 * p] for p in range(slabs // 2)],
        scratch=[pltpu.VMEM((max(slabs // 2 - 1, 1), kept, size, size), F32), pltpu.VMEM((size, 2 * size), F32)],
    )

    shares = call(
        functools.partial(share_kernel, group), jax.ShapeDtypeStruct((group, 3, 8, 128), F32), [SMEM, SMEM],
        offsets, weights,
    )
    sums = call(functools.partial(smear_kernel, group), [block] * group, [VMEM] * 4, shares, own, other_a, other_b)

    def propagate(state, slot, field):
        kernel = functools.partial(field_kernel, slabs, slot, bool(state))
        return (call(kernel, block, [VMEM] * (3 + len(state)), field, *factors, *state),)

    if group == 2 and len(chip_bits) == 1:
        bit = chip_bits[0]
        both = [
            (e * slabs + s, (e ^ 1) * slabs + (s ^ bit)) for e in range(energies) for s in range(slabs)
        ]
        near = lax.ppermute(sums[1], "energy", [(e, e ^ 1) for e in range(energies)])
        across = exchange(sums[0], bit)
        far = lax.ppermute(sums[1], ("energy", "space"), both)
        fields = {0: call(add_kernel, block, [VMEM] * 3, sums[0], near, token)}
        fields[1] = exchange(fields[0], 1)
        state = propagate((), 0, fields[0])
        fields[bit] = call(add_kernel, block, [VMEM] * 3, across, far, state[0])
        fields[bit ^ 1] = exchange(fields[bit], 1)
        rest = [1, bit, bit ^ 1]
    else:
        field = sums[0]
        for step in range(1, group):
            pairs = [(e, e - e % group + (e + step) % group) for e in range(energies)]
            field = field + lax.ppermute(sums[step], "energy", pairs)
        fields = gather({0: field}, chip_bits + [1])
        state, rest = (), sorted(fields)
    for slot in rest:
        state = propagate(state, slot, fields[slot])
    return state[0].reshape(lesser_prev.shape)


def solution(mesh):
    placed = (
        P(None, "energy", "space", None, None),
        P(None, "energy", "space", None, None),
        P(None, "space", None, None),
        P(),
        P(),
        P(),
        P(),
    )
    return jax.shard_map(
        per_device,
        mesh=mesh,
        in_specs=placed,
        out_specs=P(None, "energy", "space", None, None),
        check_vma=False,
    )
```

```python
import functools

import jax
import jax.numpy as jnp
from jax import lax
from jax.experimental import pallas as pl
from jax.experimental.pallas import tpu as pltpu
from jax.sharding import PartitionSpec as P

F32 = jnp.float32
BF16 = jnp.bfloat16
VMEM = pl.BlockSpec(memory_space=pltpu.VMEM)
SMEM = pl.BlockSpec(memory_space=pltpu.SMEM)
NN = (((1,), (0,)), ((), ()))
NT = (((1,), (1,)), ((), ()))


def split(value):
    high = value.astype(BF16)
    return high, (value - high.astype(F32)).astype(BF16)


def rows(block):
    return jnp.concatenate([block[0], block[1]], axis=1)


def block_of(row):
    half = row.shape[1] // 2
    return jnp.stack([row[:, :half], row[:, half:]])


def full(row):
    half = row.shape[1] // 2
    turned = jnp.concatenate([-row[:, half:], row[:, :half]], axis=1)
    return jnp.concatenate([row, turned], axis=0)


def product(left, right, dims):
    def dot(a, b):
        return lax.dot_general(a, b, dims, preferred_element_type=F32)

    return dot(left[0], right[0]) + (dot(left[0], right[1]) + dot(left[1], right[0]))


def times(left, right_block):
    return product(left, [full(part) for part in split(rows(right_block))], NN)


def times_dagger(left, right_block):
    return product(left, [full(part) for part in split(rows(right_block))], NT)


def share_kernel(group, offsets, weights, out):
    count = lax.axis_size("energy")
    mine = lax.axis_index("energy")
    place, rank = mine // group, mine % group
    source_a, source_b, has_a, has_b = partners(place, count // group, mine, group)

    def coefficient(target, source, valid):
        total = jnp.float32(0)
        for mode in range(offsets.shape[0]):
            total += jnp.where(target + offsets[mode] == source, weights[mode], jnp.float32(0))
        return jnp.where(valid, total, jnp.float32(0))

    for step in range(group):
        target = place * group + (rank + step) % group
        for index, (source, valid) in enumerate(((mine, True), (source_a, has_a), (source_b, has_b))):
            out[step, index] = jnp.full(out.shape[2:], coefficient(target, source, valid), F32)


def smear_kernel(group, shares, own, other_a, other_b, *outs):
    shape = (-1,) + shares.shape[2:]
    parts = [part[...].reshape(shape) for part in (own, other_a, other_b)]
    for step in range(group):
        total = sum(shares[step, index][None] * part for index, part in enumerate(parts))
        outs[step][...] = total.reshape(outs[step].shape)


def partners(place, places, mine, group):
    even = place % 2 == 0
    side_a = jnp.where(even, 1, -1)
    has_a = (place + side_a < places) & (place + side_a >= 0)
    has_b = (place - side_a < places) & (place - side_a >= 0)
    return mine + side_a * group, mine - side_a * group, has_a, has_b


def matchings(places, group):
    result = []
    for first in (0, 1):
        pairs = []
        for place in range(places):
            other = place + 1 if place % 2 == first else place - 1
            for rank in range(group):
                mine = place * group + rank
                if 0 <= other < places:
                    pairs.append((mine, other * group + rank))
                elif group % 2 == 0:
                    pairs.append((mine, mine ^ 1))
        result.append(pairs)
    return result


def pair_kernel(own_r, own_c, other_r, other_c, combined, second_r, first_c):
    odd = lax.axis_index("space") % 2 == 1
    first_r = jnp.where(odd, other_r[...], own_r[...])
    second_c = jnp.where(odd, own_c[...], other_c[...])
    second_r[...] = jnp.where(odd, own_r[...], other_r[...])
    first_c[...] = jnp.where(odd, other_c[...], own_c[...])
    combined[...] = block_of(times(split(times(split(rows(second_r)), second_c)), first_r))


def valid_terms(slab, mine, count):
    return slab <= mine, (slab >= 1) & (slab <= mine + 1), slab < mine


def factor_kernel(count, material, table, own_r, *refs):
    combined, second_r, first_c = (refs[n * count // 2 : (n + 1) * count // 2] for n in range(3))
    *outs, held, base = refs[3 * count // 2 :]
    mine = lax.axis_index("space")
    size = table.shape[-1]
    for slot in range(1, count // 2):
        for index, blocks in enumerate((combined, second_r, first_c)):
            held[slot - 1, index] = blocks[slot][...]

    def store(slab, which, parts):
        valid = valid_terms(slab, mine, count)
        position = sum((v.astype(jnp.int32) for v in valid[:which]), jnp.int32(0))

        @pl.when(valid[which] & (slab >= 0) & (slab < count))
        def _():
            for out, part in zip(outs, parts):
                out[jnp.bitwise_xor(mine, slab), pl.ds(pl.multiple_of(position * size, size), size)] = part

    def spread(slabs, maps):
        made = []
        for slab, whole in zip(slabs, maps):
            parts = split(whole)
            right = times(parts, table[material[slab]])
            left = times_dagger(parts, table[material[jnp.maximum(slab - 1, 0)]])
            made.append((parts, split(right), split(left)))
        for slab, (same, right, left) in zip(slabs, made):
            store(slab, 0, same)
            store(slab + 1, 1, right)
            store(slab - 1, 2, left)

    odd = mine % 2 == 1

    @pl.when(odd)
    def _():
        spread([mine, mine - 1], [rows(own_r), rows(combined[0])])

    @pl.when(jnp.logical_not(odd))
    def _():
        spread([mine], [rows(own_r)])

    @pl.when(mine >= 2)
    def _():
        start = split(jnp.where(odd, rows(combined[0]), rows(own_r)))
        base[...] = times(start, first_c[0])

    def earlier(step, _):
        pair = mine // 2 - step
        block = held.at[jnp.bitwise_xor(mine // 2, pair) - 1]
        parts = split(base[...])
        near, far = times(parts, block[1]), times(parts, block[0])
        spread([2 * pair + 1, 2 * pair], [near, far])
        if count > 4:
            base[...] = times(split(far), block[2])
        return _

    lax.fori_loop(1, mine // 2 + 1, earlier, 0)


def pass_kernel(value, after, out):
    out[...] = value[...]


def field_kernel(count, slots, has_state, *refs):
    fields, (high, low), rest = refs[: len(slots)], refs[len(slots) : len(slots) + 2], refs[len(slots) + 2 :]
    out = rest[-1]
    size = out.shape[-1]
    mine = lax.axis_index("space")

    def run(present):
        total = rows(rest[0]) if has_state else jnp.zeros((size, 2 * size), F32)
        for slot, field, terms in zip(slots, fields, present):
            if not terms:
                continue
            factors = [part[slot, : terms * size] for part in (high, low)]
            left = split(times(factors, field))
            for term in range(terms):
                here = slice(term * size, (term + 1) * size)
                total = total + product([p[here] for p in left], [full(f[here]) for f in factors], NT)
        out[...] = block_of(total)

    cases = {}
    for device in range(count):
        present = tuple(sum(map(bool, valid_terms(device ^ slot, device, count))) for slot in slots)
        cases.setdefault(present, []).append(device)
    for present, devices in cases.items():
        pl.when(functools.reduce(jnp.logical_or, [mine == device for device in devices]))(
            functools.partial(run, present)
        )


def call(kernel, shapes, specs, *args, scratch=()):
    return pl.pallas_call(
        kernel,
        out_shape=shapes,
        in_specs=specs,
        out_specs=jax.tree.map(lambda _: VMEM, shapes),
        scratch_shapes=scratch,
        compiler_params=pltpu.CompilerParams(vmem_limit_bytes=32 * 2**20),
        cost_estimate=pl.CostEstimate(
            flops=10**9, bytes_accessed=sum(a.size * a.dtype.itemsize for a in args), transcendentals=0
        ),
    )(*args)


def exchange(value, bit):
    count = lax.axis_size("space")
    return lax.ppermute(value, "space", [(i, i ^ bit) for i in range(count)])


def gather(slots, bits):
    for bit in bits:
        slots = slots | {key ^ bit: exchange(block, bit) for key, block in slots.items()}
    return slots


def per_device(lesser_prev, retarded, coupling, gradient_table, material, offsets, weights):
    size = lesser_prev.shape[-1]
    energies, slabs = lax.axis_size("energy"), lax.axis_size("space")
    group = max(energies // 4, 1)
    block = jax.ShapeDtypeStruct((2, size, size), F32)
    own = lesser_prev.reshape(2, size, size)
    chip_bits = [1 << b for b in range(1, slabs.bit_length() - 1)]

    pairs_a, pairs_b = matchings(energies // group, group)
    other_a = lax.ppermute(own, "energy", pairs_a)
    other_b = lax.ppermute(own, "energy", pairs_b)
    retarded = retarded.reshape(2, size, size)
    coupling = coupling.reshape(2, size, size)
    shares = call(
        functools.partial(share_kernel, group), jax.ShapeDtypeStruct((group, 3, 8, 128), F32), [SMEM] * 2,
        offsets, weights,
    )
    pair = call(
        pair_kernel, [block] * 3, [VMEM] * 4, retarded, coupling, exchange(retarded, 1), exchange(coupling, 1)
    )
    combined, second_r = (gather({0: part}, chip_bits) for part in pair[:2])
    first_c = gather({0: pair[2]}, chip_bits) if slabs > 4 else {2 * p: pair[2] for p in range(slabs // 2)}
    factor_shape = jax.ShapeDtypeStruct((slabs, 3 * size, 2 * size), BF16)
    earlier = [part[2 * p] for part in (combined, second_r, first_c) for p in range(slabs // 2)]
    factors = call(
        functools.partial(factor_kernel, slabs), [factor_shape] * 2,
        [SMEM] + [VMEM] * (2 + len(earlier)), material, gradient_table, retarded, *earlier,
        scratch=[pltpu.VMEM((max(slabs // 2 - 1, 1), 3, 2, size, size), F32), pltpu.VMEM((size, 2 * size), F32)],
    )

    sums = call(functools.partial(smear_kernel, group), [block] * group, [VMEM] * 4, shares, own, other_a, other_b)

    field = sums[0]
    for step in range(1, group):
        pairs = [(e, e - e % group + (e + step) % group) for e in range(energies)]
        arrived = lax.ppermute(sums[step], "energy", pairs)
        field = field + arrived

    def propagate(slots, fields, *state):
        kernel = functools.partial(field_kernel, slabs, slots, bool(state))
        operands = *[fields[slot] for slot in slots], *factors, *state
        return call(kernel, block, [VMEM] * len(operands), *operands)

    fields = gather({0: field}, [1])
    state = propagate([0, 1], fields)
    for bit in chip_bits:
        keys = sorted(key for key in fields if key % 2 == 0)
        for key in keys:
            arrived = call(pass_kernel, block, [VMEM] * 2, exchange(fields[key], bit), state)
            fields |= {key ^ bit: arrived, key ^ bit ^ 1: exchange(arrived, 1)}
        state = propagate([key ^ bit for key in keys], fields, state)
        state = propagate([key ^ bit ^ 1 for key in keys], fields, state)
    return state.reshape(lesser_prev.shape)


def solution(mesh):
    placed = (
        P(None, "energy", "space", None, None),
        P(None, "energy", "space", None, None),
        P(None, "space", None, None),
        P(),
        P(),
        P(),
        P(),
    )
    return jax.shard_map(
        per_device,
        mesh=mesh,
        in_specs=placed,
        out_specs=P(None, "energy", "space", None, None),
        check_vma=False,
    )
```

```python
import functools

import jax
import jax.numpy as jnp
from jax import lax
from jax.experimental import pallas as pl
from jax.experimental.pallas import tpu as pltpu
from jax.sharding import PartitionSpec as P

F32 = jnp.float32
BF16 = jnp.bfloat16
VMEM = pl.BlockSpec(memory_space=pltpu.VMEM)
SMEM = pl.BlockSpec(memory_space=pltpu.SMEM)
NN = (((1,), (0,)), ((), ()))
NT = (((1,), (1,)), ((), ()))


def split(value):
    high = value.astype(BF16)
    return high, (value - high.astype(F32)).astype(BF16)


def rows(block):
    return jnp.concatenate([block[0], block[1]], axis=1)


def block_of(row):
    half = row.shape[1] // 2
    return jnp.stack([row[:, :half], row[:, half:]])


def full(row):
    half = row.shape[1] // 2
    turned = jnp.concatenate([-row[:, half:], row[:, :half]], axis=1)
    return jnp.concatenate([row, turned], axis=0)


def product(left, right, dims):
    def dot(a, b):
        return lax.dot_general(a, b, dims, preferred_element_type=F32)

    return dot(left[0], right[0]) + (dot(left[0], right[1]) + dot(left[1], right[0]))


def times(left, right_block):
    return product(left, [full(part) for part in split(rows(right_block))], NN)


def times_dagger(left, right_block):
    return product(left, [full(part) for part in split(rows(right_block))], NT)


def share_kernel(group, offsets, weights, material, out, kinds):
    count = lax.axis_size("energy")
    mine = lax.axis_index("energy")
    place, rank = mine // group, mine % group
    source_a, source_b, has_a, has_b = partners(place, count // group, mine, group)

    def coefficient(target, source, valid):
        total = jnp.float32(0)
        for mode in range(offsets.shape[0]):
            total += jnp.where(target + offsets[mode] == source, weights[mode], jnp.float32(0))
        return jnp.where(valid, total, jnp.float32(0))

    for step in range(group):
        target = place * group + (rank + step) % group
        for index, (source, valid) in enumerate(((mine, True), (source_a, has_a), (source_b, has_b))):
            out[step, index] = jnp.full(out.shape[2:], coefficient(target, source, valid), F32)
    for slab in range(material.shape[0]):
        kinds[slab] = jnp.full(kinds.shape[1:], material[slab], jnp.int32)


def smear_kernel(group, shares, own, other_a, other_b, *outs):
    shape = (-1,) + shares.shape[2:]
    parts = [part[...].reshape(shape) for part in (own, other_a, other_b)]
    for step in range(group):
        total = sum(shares[step, index][None] * part for index, part in enumerate(parts))
        outs[step][...] = total.reshape(outs[step].shape)


def partners(place, places, mine, group):
    even = place % 2 == 0
    side_a = jnp.where(even, 1, -1)
    has_a = (place + side_a < places) & (place + side_a >= 0)
    has_b = (place - side_a < places) & (place - side_a >= 0)
    return mine + side_a * group, mine - side_a * group, has_a, has_b


def matchings(places, group):
    result = []
    for first in (0, 1):
        pairs = []
        for place in range(places):
            other = place + 1 if place % 2 == first else place - 1
            for rank in range(group):
                mine = place * group + rank
                if 0 <= other < places:
                    pairs.append((mine, other * group + rank))
                elif group % 2 == 0:
                    pairs.append((mine, mine ^ 1))
        result.append(pairs)
    return result


def pair_kernel(own_r, own_c, other_r, other_c, after, combined, sent, first_c):
    odd = lax.axis_index("space") % 2 == 1
    first_r = jnp.where(odd, other_r[...], own_r[...])
    second_r = jnp.where(odd, own_r[...], other_r[...])
    second_c = jnp.where(odd, own_c[...], other_c[...])
    first_c[...] = jnp.where(odd, other_c[...], own_c[...])
    made = block_of(times(split(times(split(rows(second_r)), second_c)), first_r))
    combined[...] = made
    sent[...] = jnp.where(odd, own_r[...], made)


def valid_terms(slab, mine, count):
    return slab <= mine, (slab >= 1) & (slab <= mine + 1), slab < mine


def factor_kernel(count, kinds, table, own_r, combined, own_first_c, *refs):
    pairs = count // 2
    sent, crossed, first_c = (refs[n * (pairs - 1) : (n + 1) * (pairs - 1)] for n in range(3))
    *outs, held, base = refs[3 * (pairs - 1) :]
    mine = lax.axis_index("space")
    odd = mine % 2 == 1
    size = table.shape[-1]
    for slot in range(pairs - 1):
        here, there = sent[slot][...], crossed[slot][...]
        held[slot, 0] = jnp.where(odd, there, here)
        held[slot, 1] = jnp.where(odd, here, there)
        held[slot, 2] = first_c[slot][...]

    def store(slab, which, parts):
        valid = valid_terms(slab, mine, count)
        position = sum((v.astype(jnp.int32) for v in valid[:which]), jnp.int32(0))

        @pl.when(valid[which] & (slab >= 0) & (slab < count))
        def _():
            for out, part in zip(outs, parts):
                out[jnp.bitwise_xor(mine, slab), pl.ds(pl.multiple_of(position * size, size), size)] = part

    def spread(slabs, maps):
        made = []
        for slab, whole in zip(slabs, maps):
            parts = split(whole)
            right = times(parts, table[kinds[slab, 0, 0]])
            left = times_dagger(parts, table[kinds[jnp.maximum(slab - 1, 0), 0, 0]])
            made.append((parts, split(right), split(left)))
        for slab, (same, right, left) in zip(slabs, made):
            store(slab, 0, same)
            store(slab + 1, 1, right)
            store(slab - 1, 2, left)

    @pl.when(odd)
    def _():
        spread([mine, mine - 1], [rows(own_r), rows(combined)])

    @pl.when(jnp.logical_not(odd))
    def _():
        spread([mine], [rows(own_r)])

    @pl.when(mine >= 2)
    def _():
        start = split(jnp.where(odd, rows(combined), rows(own_r)))
        base[...] = times(start, own_first_c)

    def earlier(step, _):
        pair = mine // 2 - step
        block = held.at[jnp.bitwise_xor(mine // 2, pair) - 1]
        parts = split(base[...])
        near, far = times(parts, block[1]), times(parts, block[0])
        spread([2 * pair + 1, 2 * pair], [near, far])
        if count > 4:
            base[...] = times(split(far), block[2])
        return _

    lax.fori_loop(1, mine // 2 + 1, earlier, 0)


def pass_kernel(value, after, out):
    out[...] = value[...]


def field_kernel(count, slots, has_state, *refs):
    fields, (high, low), rest = refs[: len(slots)], refs[len(slots) : len(slots) + 2], refs[len(slots) + 2 :]
    out = rest[-1]
    size = out.shape[-1]
    mine = lax.axis_index("space")

    def run(present):
        total = rows(rest[0]) if has_state else jnp.zeros((size, 2 * size), F32)
        for slot, field, terms in zip(slots, fields, present):
            if not terms:
                continue
            factors = [part[slot, : terms * size] for part in (high, low)]
            left = split(times(factors, field))
            for term in range(terms):
                here = slice(term * size, (term + 1) * size)
                total = total + product([p[here] for p in left], [full(f[here]) for f in factors], NT)
        out[...] = block_of(total)

    cases = {}
    for device in range(count):
        present = tuple(sum(map(bool, valid_terms(device ^ slot, device, count))) for slot in slots)
        cases.setdefault(present, []).append(device)
    for present, devices in cases.items():
        pl.when(functools.reduce(jnp.logical_or, [mine == device for device in devices]))(
            functools.partial(run, present)
        )


def call(kernel, shapes, specs, *args, scratch=()):
    return pl.pallas_call(
        kernel,
        out_shape=shapes,
        in_specs=specs,
        out_specs=jax.tree.map(lambda _: VMEM, shapes),
        scratch_shapes=scratch,
        compiler_params=pltpu.CompilerParams(vmem_limit_bytes=32 * 2**20),
        cost_estimate=pl.CostEstimate(
            flops=10**9, bytes_accessed=sum(a.size * a.dtype.itemsize for a in args), transcendentals=0
        ),
    )(*args)


def exchange(value, bit):
    count = lax.axis_size("space")
    return lax.ppermute(value, "space", [(i, i ^ bit) for i in range(count)])


def gather(slots, bits):
    for bit in bits:
        slots = slots | {key ^ bit: exchange(block, bit) for key, block in slots.items()}
    return slots


def per_device(lesser_prev, retarded, coupling, gradient_table, material, offsets, weights):
    size = lesser_prev.shape[-1]
    energies, slabs = lax.axis_size("energy"), lax.axis_size("space")
    group = max(energies // 4, 1)
    block = jax.ShapeDtypeStruct((2, size, size), F32)
    own = lesser_prev.reshape(2, size, size)
    chip_bits = [1 << b for b in range(1, slabs.bit_length() - 1)]

    pairs_a, pairs_b = matchings(energies // group, group)
    other_a = lax.ppermute(own, "energy", pairs_a)
    other_b = lax.ppermute(own, "energy", pairs_b)
    retarded = retarded.reshape(2, size, size)
    coupling = coupling.reshape(2, size, size)
    shares, kinds = call(
        functools.partial(share_kernel, group),
        [jax.ShapeDtypeStruct((group, 3, 8, 128), F32), jax.ShapeDtypeStruct((slabs, 8, 128), jnp.int32)], [SMEM] * 3,
        offsets, weights, material,
    )
    combined, sent, first_c = call(
        pair_kernel, [block] * 3, [VMEM] * 5, retarded, coupling, exchange(retarded, 1), exchange(coupling, 1), shares,
    )
    sent = gather({0: sent}, chip_bits)
    all_c = gather({0: first_c}, chip_bits) if slabs > 4 else {slot: first_c for slot in sent}
    others = [slot for slot in sorted(sent) if slot]
    earlier = (
        [sent[slot] for slot in others]
        + [exchange(sent[slot], 1) for slot in others]
        + [all_c[slot] for slot in others]
    )
    sums = call(functools.partial(smear_kernel, group), [block] * group, [VMEM] * 4, shares, own, other_a, other_b)

    field = sums[0]
    for step in range(1, group):
        pairs = [(e, e - e % group + (e + step) % group) for e in range(energies)]
        arrived = lax.ppermute(sums[step], "energy", pairs)
        field = field + arrived

    factor_shape = jax.ShapeDtypeStruct((slabs, 3 * size, 2 * size), BF16)
    factors = call(
        functools.partial(factor_kernel, slabs), [factor_shape] * 2,
        [VMEM] * (5 + len(earlier)), kinds, gradient_table, retarded, combined, first_c, *earlier,
        scratch=[pltpu.VMEM((max(slabs // 2 - 1, 1), 3, 2, size, size), F32), pltpu.VMEM((size, 2 * size), F32)],
    )

    def propagate(slots, fields, *state):
        kernel = functools.partial(field_kernel, slabs, slots, bool(state))
        operands = *[fields[slot] for slot in slots], *factors, *state
        return call(kernel, block, [VMEM] * len(operands), *operands)

    fields = {0: field}
    state = propagate([0], fields)
    own = call(pass_kernel, block, [VMEM] * 2, field, state)
    fields[1] = exchange(own, 1)
    for bit in chip_bits:
        for key in [key for key in fields if key % 2 == 0]:
            fields[key ^ bit] = call(pass_kernel, block, [VMEM] * 2, exchange(fields[key], bit), own)
    others = [key for key in sorted(fields) if key % 2 == 0 and key]
    fields |= gather({key: fields[key] for key in others}, [1])
    state = propagate([1] + others, fields, state)
    state = propagate([key ^ 1 for key in others], fields, state)
    return state.reshape(lesser_prev.shape)


def solution(mesh):
    placed = (
        P(None, "energy", "space", None, None),
        P(None, "energy", "space", None, None),
        P(None, "space", None, None),
        P(),
        P(),
        P(),
        P(),
    )
    return jax.shard_map(
        per_device,
        mesh=mesh,
        in_specs=placed,
        out_specs=P(None, "energy", "space", None, None),
        check_vma=False,
    )
```

```python
import functools

import jax
import jax.numpy as jnp
from jax import lax
from jax.experimental import pallas as pl
from jax.experimental.pallas import tpu as pltpu
from jax.sharding import PartitionSpec as P

F32 = jnp.float32
BF16 = jnp.bfloat16
VMEM = pl.BlockSpec(memory_space=pltpu.VMEM)
SMEM = pl.BlockSpec(memory_space=pltpu.SMEM)
NN = (((1,), (0,)), ((), ()))
NT = (((1,), (1,)), ((), ()))


def split(value):
    high = value.astype(BF16)
    return high, (value - high.astype(F32)).astype(BF16)


def rows(block):
    return jnp.concatenate([block[0], block[1]], axis=1)


def block_of(row):
    half = row.shape[1] // 2
    return jnp.stack([row[:, :half], row[:, half:]])


def full(row):
    half = row.shape[1] // 2
    turned = jnp.concatenate([-row[:, half:], row[:, :half]], axis=1)
    return jnp.concatenate([row, turned], axis=0)


def product(left, right, dims):
    def dot(a, b):
        return lax.dot_general(a, b, dims, preferred_element_type=F32)

    return dot(left[0], right[0]) + (dot(left[0], right[1]) + dot(left[1], right[0]))


def times(left, right_block):
    return product(left, [full(part) for part in split(rows(right_block))], NN)


def times_dagger(left, right_block):
    return product(left, [full(part) for part in split(rows(right_block))], NT)


def share_kernel(group, offsets, weights, material, out, kinds):
    count = lax.axis_size("energy")
    mine = lax.axis_index("energy")
    place, rank = mine // group, mine % group
    source_a, source_b, has_a, has_b = partners(place, count // group, mine, group)

    def coefficient(target, source, valid):
        total = jnp.float32(0)
        for mode in range(offsets.shape[0]):
            total += jnp.where(target + offsets[mode] == source, weights[mode], jnp.float32(0))
        return jnp.where(valid, total, jnp.float32(0))

    for step in range(group):
        target = place * group + (rank + step) % group
        for index, (source, valid) in enumerate(((mine, True), (source_a, has_a), (source_b, has_b))):
            out[step, index] = jnp.full(out.shape[2:], coefficient(target, source, valid), F32)
    for slab in range(material.shape[0]):
        kinds[slab] = jnp.full(kinds.shape[1:], material[slab], jnp.int32)


def smear_kernel(group, shares, own, other_a, other_b, *outs):
    shape = (-1,) + shares.shape[2:]
    parts = [part[...].reshape(shape) for part in (own, other_a, other_b)]
    for step in range(group):
        total = sum(shares[step, index][None] * part for index, part in enumerate(parts))
        outs[step][...] = total.reshape(outs[step].shape)


def partners(place, places, mine, group):
    even = place % 2 == 0
    side_a = jnp.where(even, 1, -1)
    has_a = (place + side_a < places) & (place + side_a >= 0)
    has_b = (place - side_a < places) & (place - side_a >= 0)
    return mine + side_a * group, mine - side_a * group, has_a, has_b


def matchings(places, group, slabs):
    result = []
    for first in (0, 1):
        pairs = []
        for place in range(places):
            other = place + 1 if place % 2 == first else place - 1
            for rank in range(group):
                for slab in range(slabs):
                    mine = (place * group + rank) * slabs + slab
                    inside = 0 <= other < places
                    pairs.append((mine, (other * group + rank) * slabs + slab if inside else mine ^ 1))
        result.append(pairs)
    return result


def pair_kernel(own_r, own_c, other_r, other_c, after, combined, sent, first_c):
    odd = lax.axis_index("space") % 2 == 1
    first_r = jnp.where(odd, other_r[...], own_r[...])
    second_r = jnp.where(odd, own_r[...], other_r[...])
    second_c = jnp.where(odd, own_c[...], other_c[...])
    first_c[...] = jnp.where(odd, other_c[...], own_c[...])
    made = block_of(times(split(times(split(rows(second_r)), second_c)), first_r))
    combined[...] = made
    sent[...] = jnp.where(odd, own_r[...], made)


def valid_terms(slab, mine, count):
    return slab <= mine, (slab >= 1) & (slab <= mine + 1), slab < mine


def factor_kernel(count, kinds, table, own_r, combined, own_first_c, *refs):
    pairs = count // 2
    sent, crossed, first_c = (refs[n * (pairs - 1) : (n + 1) * (pairs - 1)] for n in range(3))
    field, *outs, state, field_out, held, base = refs[3 * (pairs - 1) :]
    mine = lax.axis_index("space")
    odd = mine % 2 == 1
    size = table.shape[-1]
    for slot in range(pairs - 1):
        here, there = sent[slot][...], crossed[slot][...]
        held[slot, 0] = jnp.where(odd, there, here)
        held[slot, 1] = jnp.where(odd, here, there)
        held[slot, 2] = first_c[slot][...]

    def store(slab, which, parts):
        valid = valid_terms(slab, mine, count)
        position = sum((v.astype(jnp.int32) for v in valid[:which]), jnp.int32(0))

        @pl.when(valid[which] & (slab >= 0) & (slab < count))
        def _():
            for out, part in zip(outs, parts):
                out[jnp.bitwise_xor(mine, slab), pl.ds(pl.multiple_of(position * size, size), size)] = part

    def spread(slabs, maps):
        made = []
        for slab, whole in zip(slabs, maps):
            parts = split(whole)
            right = times(parts, table[kinds[slab, 0, 0]])
            left = times_dagger(parts, table[kinds[jnp.maximum(slab - 1, 0), 0, 0]])
            made.append((parts, split(right), split(left)))
        for slab, (same, right, left) in zip(slabs, made):
            store(slab, 0, same)
            store(slab + 1, 1, right)
            store(slab - 1, 2, left)

    @pl.when(odd)
    def _():
        spread([mine, mine - 1], [rows(own_r), rows(combined)])

    @pl.when(jnp.logical_not(odd))
    def _():
        spread([mine], [rows(own_r)])

    @pl.when(mine >= 2)
    def _():
        start = split(jnp.where(odd, rows(combined), rows(own_r)))
        base[...] = times(start, own_first_c)

    def earlier(step, _):
        pair = mine // 2 - step
        block = held.at[jnp.bitwise_xor(mine // 2, pair) - 1]
        parts = split(base[...])
        near, far = times(parts, block[1]), times(parts, block[0])
        spread([2 * pair + 1, 2 * pair], [near, far])
        if count > 4:
            base[...] = times(split(far), block[2])
        return _

    lax.fori_loop(1, mine // 2 + 1, earlier, 0)
    field_out[...] = field[...]
    add_fields(count, {0: field}, outs, None, state)


def add_fields(count, fields, factors, before, out, wanted=lambda slot, device: True):
    size = out.shape[-1]
    mine = lax.axis_index("space")

    def run(present):
        total = jnp.zeros((size, 2 * size), F32) if before is None else rows(before)
        for slot, terms in present:
            maps = [part[slot, : terms * size] for part in factors]
            left = split(times(maps, fields[slot]))
            for term in range(terms):
                here = slice(term * size, (term + 1) * size)
                total = total + product([p[here] for p in left], [full(m[here]) for m in maps], NT)
        out[...] = block_of(total)

    cases = {}
    for device in range(count):
        terms = {slot: sum(map(bool, valid_terms(device ^ slot, device, count))) for slot in fields}
        present = tuple((slot, number) for slot, number in terms.items() if number and wanted(slot, device))
        cases.setdefault(present, []).append(device)
    for present, devices in cases.items():
        here = functools.reduce(jnp.logical_or, [mine == device for device in devices])
        pl.when(here)(functools.partial(run, present))


def first_kernel(count, arrived, other, high, low, before, arrived_out, out):
    arrived_out[...] = arrived[...]
    add_fields(count, {1: other}, (high, low), before, out, lambda slot, device: device % 2 == 1)


def field_kernel(count, slots, high, low, before, *refs):
    fields = dict(zip(slots, refs))
    add_fields(count, fields, (high, low), before, refs[-1], lambda slot, device: slot != 1 or device % 2 == 0)


def call(kernel, shapes, specs, *args, scratch=()):
    return pl.pallas_call(
        kernel,
        out_shape=shapes,
        in_specs=specs,
        out_specs=jax.tree.map(lambda _: VMEM, shapes),
        scratch_shapes=scratch,
        compiler_params=pltpu.CompilerParams(vmem_limit_bytes=32 * 2**20),
        cost_estimate=pl.CostEstimate(
            flops=10**9, bytes_accessed=sum(a.size * a.dtype.itemsize for a in args), transcendentals=0
        ),
    )(*args)


def exchange(value, bit):
    count = lax.axis_size("space")
    return lax.ppermute(value, "space", [(i, i ^ bit) for i in range(count)])


def gather(slots, bits):
    for bit in bits:
        slots = slots | {key ^ bit: exchange(block, bit) for key, block in slots.items()}
    return slots


def per_device(lesser_prev, retarded, coupling, gradient_table, material, offsets, weights):
    size = lesser_prev.shape[-1]
    energies, slabs = lax.axis_size("energy"), lax.axis_size("space")
    group = max(energies // 4, 1)
    block = jax.ShapeDtypeStruct((2, size, size), F32)
    own = lesser_prev.reshape(2, size, size)
    chip_bits = [1 << b for b in range(1, slabs.bit_length() - 1)]

    pairs_a, pairs_b = matchings(energies // group, group, slabs)
    other_a = lax.ppermute(own, ("energy", "space"), pairs_a)
    other_b = lax.ppermute(own, ("energy", "space"), pairs_b)
    retarded = retarded.reshape(2, size, size)
    coupling = coupling.reshape(2, size, size)
    shares, kinds = call(
        functools.partial(share_kernel, group),
        [jax.ShapeDtypeStruct((group, 3, 8, 128), F32), jax.ShapeDtypeStruct((slabs, 8, 128), jnp.int32)], [SMEM] * 3,
        offsets, weights, material,
    )
    combined, sent, first_c = call(
        pair_kernel, [block] * 3, [VMEM] * 5, retarded, coupling, exchange(retarded, 1), exchange(coupling, 1), shares,
    )
    sent = gather({0: sent}, chip_bits)
    all_c = gather({0: first_c}, chip_bits) if slabs > 4 else {slot: first_c for slot in sent}
    others = [slot for slot in sorted(sent) if slot]
    earlier = (
        [sent[slot] for slot in others]
        + [exchange(sent[slot], 1) for slot in others]
        + [all_c[slot] for slot in others]
    )
    sums = call(functools.partial(smear_kernel, group), [block] * group, [VMEM] * 4, shares, own, other_a, other_b)

    field = sums[0]
    for step in range(1, group):
        pairs = [(e, e - e % group + (e + step) % group) for e in range(energies)]
        arrived = lax.ppermute(sums[step], "energy", pairs)
        field = field + arrived

    factor_shape = jax.ShapeDtypeStruct((slabs, 3 * size, 2 * size), BF16)
    *factors, state, own = call(
        functools.partial(factor_kernel, slabs), [factor_shape] * 2 + [block] * 2,
        [VMEM] * (6 + len(earlier)), kinds, gradient_table, retarded, combined, first_c, *earlier, field,
        scratch=[pltpu.VMEM((max(slabs // 2 - 1, 1), 3, 2, size, size), F32), pltpu.VMEM((size, 2 * size), F32)],
    )

    def propagate(slots):
        operands = *factors, state, *[fields[slot] for slot in slots]
        return call(functools.partial(field_kernel, slabs, slots), block, [VMEM] * len(operands), *operands)

    fields = {0: field, 1: exchange(own, 1)}
    for bit in chip_bits:
        for key in [key for key in fields if key % 2 == 0]:
            fields[key ^ bit] = exchange(fields[key], bit)
            if bit == chip_bits[0]:
                fields[bit], state = call(
                    functools.partial(first_kernel, slabs), [block] * 2, [VMEM] * 5,
                    fields[bit], fields[1], *factors, state,
                )
    others = [key for key in sorted(fields) if key % 2 == 0 and key]
    fields |= gather({key: fields[key] for key in others}, [1])
    state = propagate([1] + others)
    state = propagate([key ^ 1 for key in others])
    return state.reshape(lesser_prev.shape)


def solution(mesh):
    placed = (
        P(None, "energy", "space", None, None),
        P(None, "energy", "space", None, None),
        P(None, "space", None, None),
        P(),
        P(),
        P(),
        P(),
    )
    return jax.shard_map(
        per_device,
        mesh=mesh,
        in_specs=placed,
        out_specs=P(None, "energy", "space", None, None),
        check_vma=False,
    )
```

```python
import functools

import jax
import jax.numpy as jnp
from jax import lax
from jax.experimental import pallas as pl
from jax.experimental.pallas import tpu as pltpu
from jax.sharding import PartitionSpec as P

F32 = jnp.float32
BF16 = jnp.bfloat16
VMEM = pl.BlockSpec(memory_space=pltpu.VMEM)
SMEM = pl.BlockSpec(memory_space=pltpu.SMEM)
NN = (((1,), (0,)), ((), ()))
NT = (((1,), (1,)), ((), ()))


def split(value):
    high = value.astype(BF16)
    return high, (value - high.astype(F32)).astype(BF16)


def rows(block):
    return jnp.concatenate([block[0], block[1]], axis=1)


def block_of(row):
    half = row.shape[1] // 2
    return jnp.stack([row[:, :half], row[:, half:]])


def full(row):
    half = row.shape[1] // 2
    turned = jnp.concatenate([-row[:, half:], row[:, :half]], axis=1)
    return jnp.concatenate([row, turned], axis=0)


def product(left, right, dims):
    def dot(a, b):
        return lax.dot_general(a, b, dims, preferred_element_type=F32)

    return dot(left[0], right[0]) + (dot(left[0], right[1]) + dot(left[1], right[0]))


def times(left, right_block):
    return product(left, [full(part) for part in split(rows(right_block))], NN)


def times_dagger(left, right_block):
    return product(left, [full(part) for part in split(rows(right_block))], NT)


def share_kernel(group, offsets, weights, material, out, kinds):
    count = lax.axis_size("energy")
    mine = lax.axis_index("energy")
    place, rank = mine // group, mine % group
    sources = [(mine, True)]
    for lower in range(count // group - 1):
        step = jnp.where(place == lower, group, -group)
        sources.append((mine + step, (place == lower) | (place == lower + 1)))

    def coefficient(target, source, valid):
        total = jnp.float32(0)
        for mode in range(offsets.shape[0]):
            total += jnp.where(target + offsets[mode] == source, weights[mode], jnp.float32(0))
        return jnp.where(valid, total, jnp.float32(0))

    for step in range(group):
        target = place * group + (rank + step) % group
        for index, (source, valid) in enumerate(sources):
            out[step, index] = jnp.full(out.shape[2:], coefficient(target, source, valid), F32)
    for slab in range(material.shape[0]):
        kinds[slab] = jnp.full(kinds.shape[1:], material[slab], jnp.int32)


def smear_kernel(group, shares, *refs):
    held, outs = refs[:-group], refs[-group:]
    parts = [part[...].reshape((-1,) + shares.shape[2:]) for part in held]
    for step in range(group):
        total = sum(shares[step, index][None] * part for index, part in enumerate(parts))
        outs[step][...] = total.reshape(outs[step].shape)


def matchings(places, group, slabs):
    result = []
    for lower in range(places - 1):
        pairs = []
        for place in range(places):
            other = {lower: lower + 1, lower + 1: lower}.get(place)
            for rank in range(group):
                for slab in range(slabs):
                    mine = (place * group + rank) * slabs + slab
                    pairs.append((mine, mine ^ 1 if other is None else (other * group + rank) * slabs + slab))
        result.append(pairs)
    return result


def pair_kernel(own_r, own_c, other_r, after, sent):
    odd = lax.axis_index("space") % 2 == 1

    @pl.when(odd)
    def _():
        sent[...] = block_of(times(split(times(split(rows(own_r)), own_c)), other_r))

    @pl.when(jnp.logical_not(odd))
    def _():
        sent[...] = other_r[...]


def valid_terms(slab, mine, count):
    return slab <= mine, (slab >= 1) & (slab <= mine + 1), slab < mine


def factor_kernel(count, kinds, table, own_r, own_c, other_c, combined, *refs):
    pairs = count // 2
    sent, crossed, first_c = (refs[n * (pairs - 1) : (n + 1) * (pairs - 1)] for n in range(3))
    field, *outs, state, field_out, held, base = refs[3 * (pairs - 1) :]
    mine = lax.axis_index("space")
    odd = mine % 2 == 1
    size = table.shape[-1]
    for slot in range(pairs - 1):
        here, there = sent[slot][...], crossed[slot][...]
        held[slot, 0] = jnp.where(odd, here, there)
        held[slot, 1] = jnp.where(odd, there, here)
        held[slot, 2] = first_c[slot][...]

    def store(slab, which, parts):
        valid = valid_terms(slab, mine, count)
        position = sum((v.astype(jnp.int32) for v in valid[:which]), jnp.int32(0))

        @pl.when(valid[which] & (slab >= 0) & (slab < count))
        def _():
            for out, part in zip(outs, parts):
                out[jnp.bitwise_xor(mine, slab), pl.ds(pl.multiple_of(position * size, size), size)] = part

    def spread(slabs, maps):
        made = []
        for slab, whole in zip(slabs, maps):
            parts = split(whole)
            right = times(parts, table[kinds[slab, 0, 0]])
            left = times_dagger(parts, table[kinds[jnp.maximum(slab - 1, 0), 0, 0]])
            made.append((parts, split(right), split(left)))
        for slab, (same, right, left) in zip(slabs, made):
            store(slab, 0, same)
            store(slab + 1, 1, right)
            store(slab - 1, 2, left)

    @pl.when(odd)
    def _():
        spread([mine, mine - 1], [rows(own_r), rows(combined)])

    @pl.when(jnp.logical_not(odd))
    def _():
        spread([mine], [rows(own_r)])

    @pl.when(mine >= 2)
    def _():
        start = split(jnp.where(odd, rows(combined), rows(own_r)))
        base[...] = times(start, jnp.where(odd, other_c[...], own_c[...]))

    def earlier(step, _):
        pair = mine // 2 - step
        block = held.at[jnp.bitwise_xor(mine // 2, pair) - 1]
        parts = split(base[...])
        near, far = times(parts, block[1]), times(parts, block[0])
        spread([2 * pair + 1, 2 * pair], [near, far])
        if count > 4:
            base[...] = times(split(far), block[2])
        return _

    lax.fori_loop(1, mine // 2 + 1, earlier, 0)
    field_out[...] = field[...]
    add_fields(count, {0: field}, outs, None, state)


def add_fields(count, fields, factors, before, out, wanted=lambda slot, device: True):
    size = out.shape[-1]
    mine = lax.axis_index("space")

    def run(present):
        total = jnp.zeros((size, 2 * size), F32) if before is None else rows(before)
        for slot, terms in present:
            maps = [part[slot, : terms * size] for part in factors]
            left = split(times(maps, fields[slot]))
            for term in range(terms):
                here = slice(term * size, (term + 1) * size)
                total = total + product([p[here] for p in left], [full(m[here]) for m in maps], NT)
        out[...] = block_of(total)

    cases = {}
    for device in range(count):
        terms = {slot: sum(map(bool, valid_terms(device ^ slot, device, count))) for slot in fields}
        present = tuple((slot, number) for slot, number in terms.items() if number and wanted(slot, device))
        cases.setdefault(present, []).append(device)
    for present, devices in cases.items():
        here = functools.reduce(jnp.logical_or, [mine == device for device in devices])
        pl.when(here)(functools.partial(run, present))


def first_kernel(count, arrived, other, high, low, before, arrived_out, out):
    arrived_out[...] = arrived[...]
    add_fields(count, {1: other}, (high, low), before, out, lambda slot, device: device % 2 == 1)


def field_kernel(count, slots, high, low, before, *refs):
    fields = dict(zip(slots, refs))
    add_fields(count, fields, (high, low), before, refs[-1], lambda slot, device: slot != 1 or device % 2 == 0)


def call(kernel, shapes, specs, *args, scratch=()):
    return pl.pallas_call(
        kernel,
        out_shape=shapes,
        in_specs=specs,
        out_specs=jax.tree.map(lambda _: VMEM, shapes),
        scratch_shapes=scratch,
        compiler_params=pltpu.CompilerParams(vmem_limit_bytes=32 * 2**20),
        cost_estimate=pl.CostEstimate(
            flops=10**9, bytes_accessed=sum(a.size * a.dtype.itemsize for a in args), transcendentals=0
        ),
    )(*args)


def exchange(value, bit):
    count = lax.axis_size("space")
    return lax.ppermute(value, "space", [(i, i ^ bit) for i in range(count)])


def gather(slots, bits):
    for bit in bits:
        slots = slots | {key ^ bit: exchange(block, bit) for key, block in slots.items()}
    return slots


def per_device(lesser_prev, retarded, coupling, gradient_table, material, offsets, weights):
    size = lesser_prev.shape[-1]
    energies, slabs = lax.axis_size("energy"), lax.axis_size("space")
    group = max(energies // 4, 1)
    block = jax.ShapeDtypeStruct((2, size, size), F32)
    own = lesser_prev.reshape(2, size, size)
    chip_bits = [1 << b for b in range(1, slabs.bit_length() - 1)]

    held = [own]
    for pairs in matchings(energies // group, group, slabs):
        held.append(lax.ppermute(own, ("energy", "space"), pairs))
    retarded = retarded.reshape(2, size, size)
    coupling = coupling.reshape(2, size, size)
    shares, kinds = call(
        functools.partial(share_kernel, group),
        [jax.ShapeDtypeStruct((group, len(held), 8, 128), F32), jax.ShapeDtypeStruct((slabs, 8, 128), jnp.int32)], [SMEM] * 3,
        offsets, weights, material,
    )
    other_c = exchange(coupling, 1)
    combined = call(pair_kernel, block, [VMEM] * 4, retarded, coupling, exchange(retarded, 1), shares)
    sent = gather({0: combined}, chip_bits)
    first_c = coupling
    if slabs > 4:
        first_c = jnp.where(lax.axis_index("space") % 2 == 1, other_c, coupling)
    all_c = gather({0: first_c}, chip_bits) if slabs > 4 else {slot: first_c for slot in sent}
    others = [slot for slot in sorted(sent) if slot]
    earlier = (
        [sent[slot] for slot in others]
        + [exchange(sent[slot], 1) for slot in others]
        + [all_c[slot] for slot in others]
    )
    sums = call(functools.partial(smear_kernel, group), [block] * group, [VMEM] * (1 + len(held)), shares, *held)

    field = sums[0]
    for step in range(1, group):
        pairs = [(e, e - e % group + (e + step) % group) for e in range(energies)]
        arrived = lax.ppermute(sums[step], "energy", pairs)
        field = field + arrived

    factor_shape = jax.ShapeDtypeStruct((slabs, 3 * size, 2 * size), BF16)
    *factors, state, own = call(
        functools.partial(factor_kernel, slabs), [factor_shape] * 2 + [block] * 2,
        [VMEM] * (7 + len(earlier)),
        kinds, gradient_table, retarded, coupling, other_c, combined, *earlier, field,
        scratch=[pltpu.VMEM((max(slabs // 2 - 1, 1), 3, 2, size, size), F32), pltpu.VMEM((size, 2 * size), F32)],
    )

    def propagate(slots):
        operands = *factors, state, *[fields[slot] for slot in slots]
        return call(functools.partial(field_kernel, slabs, slots), block, [VMEM] * len(operands), *operands)

    fields = {0: field, 1: exchange(own, 1)}
    for bit in chip_bits:
        for key in [key for key in fields if key % 2 == 0]:
            fields[key ^ bit] = exchange(fields[key], bit)
            if bit == chip_bits[0]:
                fields[bit], state = call(
                    functools.partial(first_kernel, slabs), [block] * 2, [VMEM] * 5,
                    fields[bit], fields[1], *factors, state,
                )
    others = [key for key in sorted(fields) if key % 2 == 0 and key]
    fields |= gather({key: fields[key] for key in others}, [1])
    state = propagate([1] + others)
    state = propagate([key ^ 1 for key in others])
    return state.reshape(lesser_prev.shape)


def solution(mesh):
    placed = (
        P(None, "energy", "space", None, None),
        P(None, "energy", "space", None, None),
        P(None, "space", None, None),
        P(),
        P(),
        P(),
        P(),
    )
    return jax.shard_map(
        per_device,
        mesh=mesh,
        in_specs=placed,
        out_specs=P(None, "energy", "space", None, None),
        check_vma=False,
    )
```

```python
import functools

import jax
import jax.numpy as jnp
from jax import lax
from jax.experimental import pallas as pl
from jax.experimental.pallas import tpu as pltpu
from jax.sharding import PartitionSpec as P

F32 = jnp.float32
BF16 = jnp.bfloat16
VMEM = pl.BlockSpec(memory_space=pltpu.VMEM)
SMEM = pl.BlockSpec(memory_space=pltpu.SMEM)
NN = (((1,), (0,)), ((), ()))
NT = (((1,), (1,)), ((), ()))


def split(value):
    high = value.astype(BF16)
    return high, (value - high.astype(F32)).astype(BF16)


def rows(block):
    return jnp.concatenate([block[0], block[1]], axis=1)


def block_of(row):
    half = row.shape[1] // 2
    return jnp.stack([row[:, :half], row[:, half:]])


def full(row):
    half = row.shape[1] // 2
    turned = jnp.concatenate([-row[:, half:], row[:, :half]], axis=1)
    return jnp.concatenate([row, turned], axis=0)


def product(left, right, dims):
    def dot(a, b):
        return lax.dot_general(a, b, dims, preferred_element_type=F32)

    return dot(left[0], right[0]) + (dot(left[0], right[1]) + dot(left[1], right[0]))


def times(left, right_block):
    return product(left, [full(part) for part in split(rows(right_block))], NN)


def times_row(left, right_row):
    return product(left, [full(part) for part in split(right_row)], NN)


def times_dagger(left, right_block):
    return product(left, [full(part) for part in split(rows(right_block))], NT)


def share_kernel(group, offsets, weights, material, out, kinds):
    count = lax.axis_size("energy")
    mine = lax.axis_index("energy")
    place, rank = mine // group, mine % group
    sources = [(mine, True)]
    for lower in range(count // group - 1):
        step = jnp.where(place == lower, group, -group)
        sources.append((mine + step, (place == lower) | (place == lower + 1)))

    def coefficient(target, source, valid):
        total = jnp.float32(0)
        for mode in range(offsets.shape[0]):
            total += jnp.where(target + offsets[mode] == source, weights[mode], jnp.float32(0))
        return jnp.where(valid, total, jnp.float32(0))

    for step in range(group):
        target = place * group + (rank + step) % group
        for index, (source, valid) in enumerate(sources):
            out[step, index] = jnp.full(out.shape[2:], coefficient(target, source, valid), F32)
    for slab in range(material.shape[0]):
        kinds[slab] = jnp.full(kinds.shape[1:], material[slab], jnp.int32)


def smear_kernel(group, shares, *refs):
    held, outs = refs[:-group], refs[-group:]
    parts = [part[...].reshape((-1,) + shares.shape[2:]) for part in held]
    for step in range(group):
        total = sum(shares[step, index][None] * part for index, part in enumerate(parts))
        outs[step][...] = total.reshape(outs[step].shape)


def matchings(places, group, slabs):
    result = []
    for lower in range(places - 1):
        pairs = []
        for place in range(places):
            other = {lower: lower + 1, lower + 1: lower}.get(place)
            for rank in range(group):
                for slab in range(slabs):
                    mine = (place * group + rank) * slabs + slab
                    pairs.append((mine, mine ^ 1 if other is None else (other * group + rank) * slabs + slab))
        result.append(pairs)
    return result


def valid_terms(slab, mine, count):
    return slab <= mine, (slab >= 1) & (slab <= mine + 1), slab < mine


def factor_kernel(count, kinds, table, field, *refs):
    retarded, coupling, outs = refs[:count], refs[count : 2 * count], refs[2 * count : 2 * count + 2]
    state, field_out, held_r, held_c, chain = refs[2 * count + 2 :]
    mine = lax.axis_index("space")
    size = table.shape[-1]

    def build(device):
        steps = {
            slab: times(split(rows(coupling[device ^ slab])), retarded[device ^ (slab - 1)])
            for slab in range(1, device + 1)
        }
        whole = rows(retarded[0])
        for slab in range(device, -1, -1):
            same = split(whole)
            made = [(slab, 0, same)]
            if slab + 1 < count:
                made.append((slab + 1, 1, split(times(same, table[kinds[slab, 0, 0]]))))
            if slab:
                made.append((slab - 1, 2, split(times_dagger(same, table[kinds[slab - 1, 0, 0]]))))
                whole = times_row(same, steps[slab])
            for target, which, parts in made:
                position = sum(map(int, valid_terms(target, device, count)[:which]))
                for out, part in zip(outs, parts):
                    out[device ^ target, position * size : (position + 1) * size] = part

    def build_any():
        for slot in range(count):
            held_r[slot] = retarded[slot][...]
            held_c[slot] = coupling[slot][...]
        chain[...] = rows(retarded[0])

        def store(slab, which, parts):
            valid = valid_terms(slab, mine, count)
            position = sum((v.astype(jnp.int32) for v in valid[:which]), jnp.int32(0))

            @pl.when(valid[which] & (slab >= 0) & (slab < count))
            def _():
                for out, part in zip(outs, parts):
                    out[jnp.bitwise_xor(mine, slab), pl.ds(pl.multiple_of(position * size, size), size)] = part

        def step(index, carry):
            slab = mine - index
            before = jnp.maximum(slab - 1, 0)
            same = split(chain[...])
            right = split(times(same, table[kinds[slab, 0, 0]]))
            left = split(times_dagger(same, table[kinds[before, 0, 0]]))
            carried = times(same, held_c[jnp.bitwise_xor(mine, slab)])
            chain[...] = times(split(carried), held_r[jnp.bitwise_xor(mine, before)])
            store(slab, 0, same)
            store(slab + 1, 1, right)
            store(slab - 1, 2, left)
            return carry

        lax.fori_loop(0, mine + 1, step, 0)

    if count <= 4:
        for device in range(count):
            pl.when(mine == device)(functools.partial(build, device))
    else:
        build_any()
    field_out[...] = field[...]
    add_fields(count, {0: field}, outs, None, state)


def add_fields(count, fields, factors, before, out, wanted=lambda slot, device: True):
    size = out.shape[-1]
    mine = lax.axis_index("space")

    def run(present):
        total = jnp.zeros((size, 2 * size), F32) if before is None else rows(before)
        for slot, terms in present:
            maps = [part[slot, : terms * size] for part in factors]
            left = split(times(maps, fields[slot]))
            for term in range(terms):
                here = slice(term * size, (term + 1) * size)
                total = total + product([p[here] for p in left], [full(m[here]) for m in maps], NT)
        out[...] = block_of(total)

    cases = {}
    for device in range(count):
        terms = {slot: sum(map(bool, valid_terms(device ^ slot, device, count))) for slot in fields}
        present = tuple((slot, number) for slot, number in terms.items() if number and wanted(slot, device))
        cases.setdefault(present, []).append(device)
    for present, devices in cases.items():
        here = functools.reduce(jnp.logical_or, [mine == device for device in devices])
        pl.when(here)(functools.partial(run, present))


def first_kernel(count, arrived, other, high, low, before, arrived_out, out):
    arrived_out[...] = arrived[...]
    add_fields(count, {1: other}, (high, low), before, out, lambda slot, device: device % 2 == 1)


def add_kernel(left, right, out):
    out[...] = left[...] + right[...]


def same_kernel(value, out):
    out[...] = value[...]


def mix_kernel(own, arrived, out):
    odd = lax.axis_index("space") % 2 == 1
    out[...] = jnp.where(odd, arrived[...], own[...])


def field_kernel(count, slots, high, low, before, *refs):
    fields = dict(zip(slots, refs))
    add_fields(count, fields, (high, low), before, refs[-1], lambda slot, device: slot != 1 or device % 2 == 0)


def call(kernel, shapes, specs, *args, scratch=()):
    return pl.pallas_call(
        kernel,
        out_shape=shapes,
        in_specs=specs,
        out_specs=jax.tree.map(lambda _: VMEM, shapes),
        scratch_shapes=scratch,
        compiler_params=pltpu.CompilerParams(vmem_limit_bytes=32 * 2**20),
        cost_estimate=pl.CostEstimate(
            flops=10**9, bytes_accessed=sum(a.size * a.dtype.itemsize for a in args), transcendentals=0
        ),
    )(*args)


def exchange(value, bit):
    count = lax.axis_size("space")
    return lax.ppermute(value, "space", [(i, i ^ bit) for i in range(count)])


def gather(slots, bits):
    for bit in bits:
        slots = slots | {key ^ bit: exchange(block, bit) for key, block in slots.items()}
    return slots


def per_device(lesser_prev, retarded, coupling, gradient_table, material, offsets, weights):
    size = lesser_prev.shape[-1]
    energies, slabs = lax.axis_size("energy"), lax.axis_size("space")
    group = max(energies // 4, 1)
    block = jax.ShapeDtypeStruct((2, size, size), F32)
    own = lesser_prev.reshape(2, size, size)
    chip_bits = [1 << b for b in range(1, slabs.bit_length() - 1)]

    held = [own]
    for pairs in matchings(energies // group, group, slabs):
        held.append(lax.ppermute(own, ("energy", "space"), pairs))
    retarded = retarded.reshape(2, size, size)
    coupling = coupling.reshape(2, size, size)
    shares, kinds = call(
        functools.partial(share_kernel, group),
        [jax.ShapeDtypeStruct((group, len(held), 8, 128), F32), jax.ShapeDtypeStruct((slabs, 8, 128), jnp.int32)], [SMEM] * 3,
        offsets, weights, material,
    )
    all_r = gather({0: retarded}, chip_bits + [1])
    if len(chip_bits) == 1:
        bit = chip_bits[0]
        arrived = exchange(coupling, bit)
        mixed = exchange(call(mix_kernel, block, [VMEM] * 2, coupling, arrived), 1)
        all_c = {0: coupling, 1: mixed, bit: arrived, bit ^ 1: mixed}
    else:
        all_c = gather({0: coupling}, chip_bits + [1])
    sums = call(functools.partial(smear_kernel, group), [block] * group, [VMEM] * (1 + len(held)), shares, *held)

    field = sums[0]
    for step in range(1, group):
        pairs = [(e, e - e % group + (e + step) % group) for e in range(energies)]
        arrived = lax.ppermute(sums[step], "energy", pairs)
        field = field + arrived

    factor_shape = jax.ShapeDtypeStruct((slabs, 3 * size, 2 * size), BF16)
    *factors, state, own = call(
        functools.partial(factor_kernel, slabs), [factor_shape] * 2 + [block] * 2, [VMEM] * (2 * slabs + 3),
        kinds, gradient_table, field, *[all_r[s] for s in range(slabs)], *[all_c[s] for s in range(slabs)],
        scratch=[pltpu.VMEM((slabs, 2, size, size), F32)] * 2 + [pltpu.VMEM((size, 2 * size), F32)],
    )

    def propagate(slots):
        operands = *factors, state, *[fields[slot] for slot in slots]
        return call(functools.partial(field_kernel, slabs, slots), block, [VMEM] * len(operands), *operands)

    fields = {0: field, 1: exchange(own, 1)}
    for bit in chip_bits:
        for key in [key for key in fields if key % 2 == 0]:
            fields[key ^ bit] = exchange(fields[key], bit)
            fields[key ^ bit] = call(same_kernel, block, [VMEM], fields[key ^ bit])
            if bit == chip_bits[0]:
                fields[bit], state = call(
                    functools.partial(first_kernel, slabs), [block] * 2, [VMEM] * 5,
                    fields[bit], fields[1], *factors, state,
                )
    others = [key for key in sorted(fields) if key % 2 == 0 and key]
    fields |= gather({key: fields[key] for key in others}, [1])
    state = propagate([1] + others)
    state = propagate([key ^ 1 for key in others])
    return state.reshape(lesser_prev.shape)


def solution(mesh):
    placed = (
        P(None, "energy", "space", None, None),
        P(None, "energy", "space", None, None),
        P(None, "space", None, None),
        P(),
        P(),
        P(),
        P(),
    )
    return jax.shard_map(
        per_device,
        mesh=mesh,
        in_specs=placed,
        out_specs=P(None, "energy", "space", None, None),
        check_vma=False,
    )
```

```python
import functools

import jax
import jax.numpy as jnp
from jax import lax
from jax.experimental import pallas as pl
from jax.experimental.pallas import tpu as pltpu
from jax.sharding import PartitionSpec as P

F32 = jnp.float32
BF16 = jnp.bfloat16
VMEM = pl.BlockSpec(memory_space=pltpu.VMEM)
SMEM = pl.BlockSpec(memory_space=pltpu.SMEM)
NN = (((1,), (0,)), ((), ()))
NT = (((1,), (1,)), ((), ()))


def split(value):
    high = value.astype(BF16)
    return high, (value - high.astype(F32)).astype(BF16)


def rows(block):
    return jnp.concatenate([block[0], block[1]], axis=1)


def block_of(row):
    half = row.shape[1] // 2
    return jnp.stack([row[:, :half], row[:, half:]])


def full(row):
    half = row.shape[1] // 2
    turned = jnp.concatenate([-row[:, half:], row[:, :half]], axis=1)
    return jnp.concatenate([row, turned], axis=0)


def product(left, right, dims):
    def dot(a, b):
        return lax.dot_general(a, b, dims, preferred_element_type=F32)

    return dot(left[0], right[0]) + (dot(left[0], right[1]) + dot(left[1], right[0]))


def times(left, right_block):
    return product(left, [full(part) for part in split(rows(right_block))], NN)


def times_row(left, right_row):
    return product(left, [full(part) for part in split(right_row)], NN)


def times_dagger(left, right_block):
    return product(left, [full(part) for part in split(rows(right_block))], NT)


def share_kernel(group, offsets, weights, material, out, kinds):
    count = lax.axis_size("energy")
    mine = lax.axis_index("energy")
    place, rank = mine // group, mine % group
    sources = [(mine, True)]
    for lower in range(count // group - 1):
        step = jnp.where(place == lower, group, -group)
        sources.append((mine + step, (place == lower) | (place == lower + 1)))

    def coefficient(target, source, valid):
        total = jnp.float32(0)
        for mode in range(offsets.shape[0]):
            total += jnp.where(target + offsets[mode] == source, weights[mode], jnp.float32(0))
        return jnp.where(valid, total, jnp.float32(0))

    for step in range(group):
        target = place * group + (rank + step) % group
        for index, (source, valid) in enumerate(sources):
            out[step, index] = jnp.full(out.shape[2:], coefficient(target, source, valid), F32)
    for slab in range(material.shape[0]):
        kinds[slab] = jnp.full(kinds.shape[1:], material[slab], jnp.int32)


def smear_kernel(group, shares, *refs):
    held, outs = refs[:-group], refs[-group:]
    parts = [part[...].reshape((-1,) + shares.shape[2:]) for part in held]
    for step in range(group):
        total = sum(shares[step, index][None] * part for index, part in enumerate(parts))
        outs[step][...] = total.reshape(outs[step].shape)


def matchings(places, group, slabs):
    result = []
    for lower in range(places - 1):
        pairs = []
        for place in range(places):
            other = {lower: lower + 1, lower + 1: lower}.get(place)
            for rank in range(group):
                for slab in range(slabs):
                    mine = (place * group + rank) * slabs + slab
                    pairs.append((mine, mine ^ 1 if other is None else (other * group + rank) * slabs + slab))
        result.append(pairs)
    return result


def valid_terms(slab, mine, count):
    return slab <= mine, (slab >= 1) & (slab <= mine + 1), slab < mine


def factor_kernel(count, kinds, table, field, *refs):
    retarded, coupling, outs = refs[:count], refs[count : 2 * count], refs[2 * count : 2 * count + 2]
    state, field_out, held_r, held_c, chain = refs[2 * count + 2 :]
    mine = lax.axis_index("space")
    size = table.shape[-1]

    def build(device):
        steps = {
            slab: times(split(rows(coupling[device ^ slab])), retarded[device ^ (slab - 1)])
            for slab in range(1, device + 1)
        }
        whole = rows(retarded[0])
        for slab in range(device, -1, -1):
            same = split(whole)
            made = [(slab, 0, same)]
            if slab + 1 < count:
                made.append((slab + 1, 1, split(times(same, table[kinds[slab, 0, 0]]))))
            if slab:
                made.append((slab - 1, 2, split(times_dagger(same, table[kinds[slab - 1, 0, 0]]))))
                whole = times_row(same, steps[slab])
            for target, which, parts in made:
                position = sum(map(int, valid_terms(target, device, count)[:which]))
                for out, part in zip(outs, parts):
                    out[device ^ target, position * size : (position + 1) * size] = part

    def build_any():
        for slot in range(count):
            held_r[slot] = retarded[slot][...]
            held_c[slot] = coupling[slot][...]
        chain[...] = rows(retarded[0])

        def store(slab, which, parts):
            valid = valid_terms(slab, mine, count)
            position = sum((v.astype(jnp.int32) for v in valid[:which]), jnp.int32(0))

            @pl.when(valid[which] & (slab >= 0) & (slab < count))
            def _():
                for out, part in zip(outs, parts):
                    out[jnp.bitwise_xor(mine, slab), pl.ds(pl.multiple_of(position * size, size), size)] = part

        def step(index, carry):
            slab = mine - index
            before = jnp.maximum(slab - 1, 0)
            same = split(chain[...])
            right = split(times(same, table[kinds[slab, 0, 0]]))
            left = split(times_dagger(same, table[kinds[before, 0, 0]]))
            carried = times(same, held_c[jnp.bitwise_xor(mine, slab)])
            chain[...] = times(split(carried), held_r[jnp.bitwise_xor(mine, before)])
            store(slab, 0, same)
            store(slab + 1, 1, right)
            store(slab - 1, 2, left)
            return carry

        lax.fori_loop(0, mine + 1, step, 0)

    if count <= 4:
        for device in range(count):
            pl.when(mine == device)(functools.partial(build, device))
    else:
        build_any()
    field_out[...] = field[...]
    add_fields(count, {0: field}, outs, None, state)


def add_fields(count, fields, factors, before, out, wanted=lambda slot, device: True):
    size = out.shape[-1]
    mine = lax.axis_index("space")

    def run(present):
        total = jnp.zeros((size, 2 * size), F32) if before is None else rows(before)
        for slot, terms in present:
            maps = [part[slot, : terms * size] for part in factors]
            left = split(times(maps, fields[slot]))
            for term in range(terms):
                here = slice(term * size, (term + 1) * size)
                total = total + product([p[here] for p in left], [full(m[here]) for m in maps], NT)
        out[...] = block_of(total)

    cases = {}
    for device in range(count):
        terms = {slot: sum(map(bool, valid_terms(device ^ slot, device, count))) for slot in fields}
        present = tuple((slot, number) for slot, number in terms.items() if number and wanted(slot, device))
        cases.setdefault(present, []).append(device)
    for present, devices in cases.items():
        here = functools.reduce(jnp.logical_or, [mine == device for device in devices])
        pl.when(here)(functools.partial(run, present))


def first_kernel(count, arrived, other, high, low, before, arrived_out, out):
    arrived_out[...] = arrived[...]
    add_fields(count, {1: other}, (high, low), before, out, lambda slot, device: device % 2 == 1)


def add_kernel(left, right, out):
    out[...] = left[...] + right[...]


def same_kernel(value, out):
    out[...] = value[...]


def pass_kernel(value, after, out):
    out[...] = value[...]


def mix_kernel(own, arrived, out):
    odd = lax.axis_index("space") % 2 == 1
    out[...] = jnp.where(odd, arrived[...], own[...])


def field_kernel(count, slots, high, low, before, *refs):
    fields = dict(zip(slots, refs))
    add_fields(count, fields, (high, low), before, refs[-1], lambda slot, device: slot != 1 or device % 2 == 0)


def call(kernel, shapes, specs, *args, scratch=()):
    return pl.pallas_call(
        kernel,
        out_shape=shapes,
        in_specs=specs,
        out_specs=jax.tree.map(lambda _: VMEM, shapes),
        scratch_shapes=scratch,
        compiler_params=pltpu.CompilerParams(vmem_limit_bytes=32 * 2**20),
        cost_estimate=pl.CostEstimate(
            flops=10**9, bytes_accessed=sum(a.size * a.dtype.itemsize for a in args), transcendentals=0
        ),
    )(*args)


def exchange(value, bit):
    count = lax.axis_size("space")
    return lax.ppermute(value, "space", [(i, i ^ bit) for i in range(count)])


def gather(slots, bits):
    for bit in bits:
        slots = slots | {key ^ bit: exchange(block, bit) for key, block in slots.items()}
    return slots


def per_device(lesser_prev, retarded, coupling, gradient_table, material, offsets, weights):
    size = lesser_prev.shape[-1]
    energies, slabs = lax.axis_size("energy"), lax.axis_size("space")
    group = max(energies // 4, 1)
    block = jax.ShapeDtypeStruct((2, size, size), F32)
    own = lesser_prev.reshape(2, size, size)
    chip_bits = [1 << b for b in range(1, slabs.bit_length() - 1)]

    held = [own]
    for pairs in matchings(energies // group, group, slabs):
        held.append(lax.ppermute(own, ("energy", "space"), pairs))
    retarded = retarded.reshape(2, size, size)
    coupling = coupling.reshape(2, size, size)
    shares, kinds = call(
        functools.partial(share_kernel, group),
        [jax.ShapeDtypeStruct((group, len(held), 8, 128), F32), jax.ShapeDtypeStruct((slabs, 8, 128), jnp.int32)], [SMEM] * 3,
        offsets, weights, material,
    )
    sums = call(functools.partial(smear_kernel, group), [block] * group, [VMEM] * (1 + len(held)), shares, *held)
    if len(chip_bits) == 1:
        bit = chip_bits[0]
        arrived = exchange(retarded, bit)
        later = call(pass_kernel, block, [VMEM] * 2, retarded, sums[0])
        all_r = {0: retarded, 1: exchange(later, 1), bit: arrived, bit ^ 1: exchange(arrived, 1)}
        pairs = [
            (e * slabs + i, e * slabs + (i ^ bit) if i % 2 or group % 2 else (e ^ 1) * slabs + i)
            for e in range(energies) for i in range(slabs)
        ]
        arrived = lax.ppermute(coupling, ("energy", "space"), pairs)
        mixed = exchange(call(mix_kernel, block, [VMEM] * 2, coupling, arrived), 1)
        all_c = {0: coupling, 1: mixed, bit: arrived, bit ^ 1: mixed}
    else:
        all_r = gather({0: retarded}, chip_bits + [1])
        all_c = gather({0: coupling}, chip_bits + [1])

    field = sums[0]
    for step in range(1, group):
        pairs = [(e, e - e % group + (e + step) % group) for e in range(energies)]
        arrived = lax.ppermute(sums[step], "energy", pairs)
        field = field + arrived

    factor_shape = jax.ShapeDtypeStruct((slabs, 3 * size, 2 * size), BF16)
    *factors, state, own = call(
        functools.partial(factor_kernel, slabs), [factor_shape] * 2 + [block] * 2, [VMEM] * (2 * slabs + 3),
        kinds, gradient_table, field, *[all_r[s] for s in range(slabs)], *[all_c[s] for s in range(slabs)],
        scratch=[pltpu.VMEM((slabs, 2, size, size), F32)] * 2 + [pltpu.VMEM((size, 2 * size), F32)],
    )

    def propagate(slots):
        operands = *factors, state, *[fields[slot] for slot in slots]
        return call(functools.partial(field_kernel, slabs, slots), block, [VMEM] * len(operands), *operands)

    fields = {0: field, 1: exchange(own, 1)}
    for bit in chip_bits:
        for key in [key for key in fields if key % 2 == 0]:
            fields[key ^ bit] = exchange(fields[key], bit)
            fields[key ^ bit] = call(same_kernel, block, [VMEM], fields[key ^ bit])
            if bit == chip_bits[0]:
                fields[bit], state = call(
                    functools.partial(first_kernel, slabs), [block] * 2, [VMEM] * 5,
                    fields[bit], fields[1], *factors, state,
                )
    others = [key for key in sorted(fields) if key % 2 == 0 and key]
    fields |= gather({key: fields[key] for key in others}, [1])
    state = propagate([1] + others)
    state = propagate([key ^ 1 for key in others])
    return state.reshape(lesser_prev.shape)


def solution(mesh):
    placed = (
        P(None, "energy", "space", None, None),
        P(None, "energy", "space", None, None),
        P(None, "space", None, None),
        P(),
        P(),
        P(),
        P(),
    )
    return jax.shard_map(
        per_device,
        mesh=mesh,
        in_specs=placed,
        out_specs=P(None, "energy", "space", None, None),
        check_vma=False,
    )
```

```python
import functools

import jax
import jax.numpy as jnp
from jax import lax
from jax.experimental import pallas as pl
from jax.experimental.pallas import tpu as pltpu
from jax.sharding import PartitionSpec as P

F32 = jnp.float32
BF16 = jnp.bfloat16
VMEM = pl.BlockSpec(memory_space=pltpu.VMEM)
SMEM = pl.BlockSpec(memory_space=pltpu.SMEM)
NN = (((1,), (0,)), ((), ()))
NT = (((1,), (1,)), ((), ()))


def split(value):
    high = value.astype(BF16)
    return high, (value - high.astype(F32)).astype(BF16)


def rows(block):
    return jnp.concatenate([block[0], block[1]], axis=1)


def block_of(row):
    half = row.shape[1] // 2
    return jnp.stack([row[:, :half], row[:, half:]])


def full(row):
    half = row.shape[1] // 2
    turned = jnp.concatenate([-row[:, half:], row[:, :half]], axis=1)
    return jnp.concatenate([row, turned], axis=0)


def product(left, right, dims):
    def dot(a, b):
        return lax.dot_general(a, b, dims, preferred_element_type=F32)

    return dot(left[0], right[0]) + (dot(left[0], right[1]) + dot(left[1], right[0]))


def times(left, right_block):
    return product(left, [full(part) for part in split(rows(right_block))], NN)


def times_row(left, right_row):
    return product(left, [full(part) for part in split(right_row)], NN)


def times_dagger(left, right_block):
    return product(left, [full(part) for part in split(rows(right_block))], NT)


def share_kernel(group, offsets, weights, material, out, kinds):
    count = lax.axis_size("energy")
    mine = lax.axis_index("energy")
    place, rank = mine // group, mine % group
    sources = [(mine, True)]
    for lower in range(count // group - 1):
        step = jnp.where(place == lower, group, -group)
        sources.append((mine + step, (place == lower) | (place == lower + 1)))

    def coefficient(target, source, valid):
        total = jnp.float32(0)
        for mode in range(offsets.shape[0]):
            total += jnp.where(target + offsets[mode] == source, weights[mode], jnp.float32(0))
        return jnp.where(valid, total, jnp.float32(0))

    for step in range(group):
        target = place * group + (rank + step) % group
        for index, (source, valid) in enumerate(sources):
            out[step, index] = jnp.full(out.shape[2:], coefficient(target, source, valid), F32)
    for slab in range(material.shape[0]):
        kinds[slab] = jnp.full(kinds.shape[1:], material[slab], jnp.int32)


def smear_kernel(group, shares, *refs):
    held, outs = refs[:-group], refs[-group:]
    parts = [part[...].reshape((-1,) + shares.shape[2:]) for part in held]
    for step in range(group):
        total = sum(shares[step, index][None] * part for index, part in enumerate(parts))
        outs[step][...] = total.reshape(outs[step].shape)


def matchings(places, group, slabs):
    result = []
    for lower in range(places - 1):
        pairs = []
        for place in range(places):
            other = {lower: lower + 1, lower + 1: lower}.get(place)
            for rank in range(group):
                for slab in range(slabs):
                    mine = (place * group + rank) * slabs + slab
                    pairs.append((mine, mine ^ 1 if other is None else (other * group + rank) * slabs + slab))
        result.append(pairs)
    return result


def valid_terms(slab, mine, count):
    return slab <= mine, (slab >= 1) & (slab <= mine + 1), slab < mine


def factor_kernel(count, kinds, table, field, *refs):
    retarded, coupling, outs = refs[:count], refs[count : 2 * count], refs[2 * count : 2 * count + 2]
    turned, (state, field_out, held_r, held_c, chain) = refs[2 * count + 2 : 2 * count + 4], refs[2 * count + 4 :]
    mine = lax.axis_index("space")
    size = table.shape[-1]

    def build(device):
        steps = {
            slab: times(split(rows(coupling[device ^ slab])), retarded[device ^ (slab - 1)])
            for slab in range(1, device + 1)
        }
        whole = rows(retarded[0])
        for slab in range(device, -1, -1):
            same = split(whole)
            made = [(slab, 0, same)]
            if slab + 1 < count:
                made.append((slab + 1, 1, split(times(same, table[kinds[slab, 0, 0]]))))
            if slab:
                made.append((slab - 1, 2, split(times_dagger(same, table[kinds[slab - 1, 0, 0]]))))
                whole = times_row(same, steps[slab])
            for target, which, parts in made:
                position = sum(map(int, valid_terms(target, device, count)[:which]))
                for out, part in zip(outs, parts):
                    out[device ^ target, position * size : (position + 1) * size] = part
                if device ^ target == count - 1:
                    for out, part in zip(turned, parts):
                        out[position] = full(part).astype(F32).T.astype(BF16)

    def build_any():
        for slot in range(count):
            held_r[slot] = retarded[slot][...]
            held_c[slot] = coupling[slot][...]
        chain[...] = rows(retarded[0])

        def store(slab, which, parts):
            valid = valid_terms(slab, mine, count)
            position = sum((v.astype(jnp.int32) for v in valid[:which]), jnp.int32(0))

            @pl.when(valid[which] & (slab >= 0) & (slab < count))
            def _():
                for out, part in zip(outs, parts):
                    out[jnp.bitwise_xor(mine, slab), pl.ds(pl.multiple_of(position * size, size), size)] = part

        def step(index, carry):
            slab = mine - index
            before = jnp.maximum(slab - 1, 0)
            same = split(chain[...])
            right = split(times(same, table[kinds[slab, 0, 0]]))
            left = split(times_dagger(same, table[kinds[before, 0, 0]]))
            carried = times(same, held_c[jnp.bitwise_xor(mine, slab)])
            chain[...] = times(split(carried), held_r[jnp.bitwise_xor(mine, before)])
            store(slab, 0, same)
            store(slab + 1, 1, right)
            store(slab - 1, 2, left)
            return carry

        lax.fori_loop(0, mine + 1, step, 0)

    if count <= 4:
        for device in range(count):
            pl.when(mine == device)(functools.partial(build, device))
    else:
        build_any()
    field_out[...] = field[...]
    add_fields(count, {0: field}, outs, None, state)


def add_fields(count, fields, factors, before, out, wanted=lambda slot, device: True, turned=None):
    size = out.shape[-1]
    mine = lax.axis_index("space")

    def run(present):
        total = jnp.zeros((size, 2 * size), F32) if before is None else rows(before)
        for slot, terms in present:
            maps = [part[slot, : terms * size] for part in factors]
            left = split(times(maps, fields[slot]))
            for term in range(terms):
                here = slice(term * size, (term + 1) * size)
                if turned is None:
                    total = total + product([p[here] for p in left], [full(m[here]) for m in maps], NT)
                else:
                    total = total + product([p[here] for p in left], [t[term] for t in turned], NN)
        out[...] = block_of(total)

    cases = {}
    for device in range(count):
        terms = {slot: sum(map(bool, valid_terms(device ^ slot, device, count))) for slot in fields}
        present = tuple((slot, number) for slot, number in terms.items() if number and wanted(slot, device))
        cases.setdefault(present, []).append(device)
    for present, devices in cases.items():
        here = functools.reduce(jnp.logical_or, [mine == device for device in devices])
        pl.when(here)(functools.partial(run, present))


def first_kernel(count, arrived, other, high, low, before, arrived_out, out):
    arrived_out[...] = arrived[...]
    add_fields(count, {1: other}, (high, low), before, out, lambda slot, device: device % 2 == 1)


def add_kernel(left, right, out):
    out[...] = left[...] + right[...]


def same_kernel(value, out):
    out[...] = value[...]


def pass_kernel(value, after, out):
    out[...] = value[...]


def mix_kernel(own, arrived, out):
    odd = lax.axis_index("space") % 2 == 1
    out[...] = jnp.where(odd, arrived[...], own[...])


def field_kernel(count, slots, high, low, before, *refs):
    fields = dict(zip(slots, refs))
    add_fields(count, fields, (high, low), before, refs[-1], lambda slot, device: slot != 1 or device % 2 == 0)


def last_kernel(count, high, low, turned_high, turned_low, before, field, out):
    add_fields(count, {count - 1: field}, (high, low), before, out, turned=(turned_high, turned_low))


def call(kernel, shapes, specs, *args, scratch=()):
    return pl.pallas_call(
        kernel,
        out_shape=shapes,
        in_specs=specs,
        out_specs=jax.tree.map(lambda _: VMEM, shapes),
        scratch_shapes=scratch,
        compiler_params=pltpu.CompilerParams(vmem_limit_bytes=32 * 2**20),
        cost_estimate=pl.CostEstimate(
            flops=10**9, bytes_accessed=sum(a.size * a.dtype.itemsize for a in args), transcendentals=0
        ),
    )(*args)


def exchange(value, bit):
    count = lax.axis_size("space")
    return lax.ppermute(value, "space", [(i, i ^ bit) for i in range(count)])


def gather(slots, bits):
    for bit in bits:
        slots = slots | {key ^ bit: exchange(block, bit) for key, block in slots.items()}
    return slots


def per_device(lesser_prev, retarded, coupling, gradient_table, material, offsets, weights):
    size = lesser_prev.shape[-1]
    energies, slabs = lax.axis_size("energy"), lax.axis_size("space")
    group = max(energies // 4, 1)
    block = jax.ShapeDtypeStruct((2, size, size), F32)
    own = lesser_prev.reshape(2, size, size)
    chip_bits = [1 << b for b in range(1, slabs.bit_length() - 1)]

    held = [own]
    for pairs in matchings(energies // group, group, slabs):
        held.append(lax.ppermute(own, ("energy", "space"), pairs))
    retarded = retarded.reshape(2, size, size)
    coupling = coupling.reshape(2, size, size)
    shares, kinds = call(
        functools.partial(share_kernel, group),
        [jax.ShapeDtypeStruct((group, len(held), 8, 128), F32), jax.ShapeDtypeStruct((slabs, 8, 128), jnp.int32)], [SMEM] * 3,
        offsets, weights, material,
    )
    sums = call(functools.partial(smear_kernel, group), [block] * group, [VMEM] * (1 + len(held)), shares, *held)
    if len(chip_bits) == 1:
        bit = chip_bits[0]
        arrived = exchange(retarded, bit)
        later = call(pass_kernel, block, [VMEM] * 2, retarded, sums[0])
        all_r = {0: retarded, 1: exchange(later, 1), bit: arrived, bit ^ 1: exchange(arrived, 1)}
        pairs = [
            (e * slabs + i, e * slabs + (i ^ bit) if i % 2 or group % 2 else (e ^ 1) * slabs + i)
            for e in range(energies) for i in range(slabs)
        ]
        arrived = lax.ppermute(coupling, ("energy", "space"), pairs)
        mixed = exchange(call(mix_kernel, block, [VMEM] * 2, coupling, arrived), 1)
        all_c = {0: coupling, 1: mixed, bit: arrived, bit ^ 1: mixed}
    else:
        all_r = gather({0: retarded}, chip_bits + [1])
        all_c = gather({0: coupling}, chip_bits + [1])

    field = sums[0]
    for step in range(1, group):
        pairs = [(e, e - e % group + (e + step) % group) for e in range(energies)]
        arrived = lax.ppermute(sums[step], "energy", pairs)
        field = field + arrived

    factor_shape = jax.ShapeDtypeStruct((slabs, 3 * size, 2 * size), BF16)
    turned_shape = jax.ShapeDtypeStruct((3, 2 * size, 2 * size), BF16)
    *factors, turned_high, turned_low, state, own = call(
        functools.partial(factor_kernel, slabs), [factor_shape] * 2 + [turned_shape] * 2 + [block] * 2, [VMEM] * (2 * slabs + 3),
        kinds, gradient_table, field, *[all_r[s] for s in range(slabs)], *[all_c[s] for s in range(slabs)],
        scratch=[pltpu.VMEM((slabs, 2, size, size), F32)] * 2 + [pltpu.VMEM((size, 2 * size), F32)],
    )

    def propagate(slots):
        operands = *factors, state, *[fields[slot] for slot in slots]
        return call(functools.partial(field_kernel, slabs, slots), block, [VMEM] * len(operands), *operands)

    fields = {0: field, 1: exchange(own, 1)}
    for bit in chip_bits:
        for key in [key for key in fields if key % 2 == 0]:
            fields[key ^ bit] = exchange(fields[key], bit)
            fields[key ^ bit] = call(same_kernel, block, [VMEM], fields[key ^ bit])
            if bit == chip_bits[0]:
                fields[bit], state = call(
                    functools.partial(first_kernel, slabs), [block] * 2, [VMEM] * 5,
                    fields[bit], fields[1], *factors, state,
                )
    others = [key for key in sorted(fields) if key % 2 == 0 and key]
    fields |= gather({key: fields[key] for key in others}, [1])
    state = propagate([1] + others)
    if slabs <= 4 and len(others) == 1:
        state = call(
            functools.partial(last_kernel, slabs), block, [VMEM] * 6,
            *factors, turned_high, turned_low, state, fields[slabs - 1],
        )
    else:
        state = propagate([key ^ 1 for key in others])
    return state.reshape(lesser_prev.shape)


def solution(mesh):
    placed = (
        P(None, "energy", "space", None, None),
        P(None, "energy", "space", None, None),
        P(None, "space", None, None),
        P(),
        P(),
        P(),
        P(),
    )
    return jax.shard_map(
        per_device,
        mesh=mesh,
        in_specs=placed,
        out_specs=P(None, "energy", "space", None, None),
        check_vma=False,
    )
```
